128 devices in a mesh: grp: 4 (over y), dev: 32 (over x, z, core).
Axes of the slice: x: 4, y: 4, z: 4, core: 2. Of those that a mesh axis runs over, the one named last changes fastest.
Arguments:
- enthalpy: float32 [128, 2048, 512], P('grp', 'dev'), may hold values from -0.5 to 1.5
- conduct: float32 [128, 2048, 512], P('grp', 'dev'), may hold values from 0.1 to 1
- tile_count: int32 [128], P(('grp', 'dev')), may hold values from 1 to 16, as said below
- tile_list: int32 [128, 16], P(('grp', 'dev')), may hold values from 0 to 255, as said below
- neighbours: int32 [1024, 6], P(('grp', 'dev')), may hold values from -1 to 1023, as said below
Outputs:
- enthalpy_next: float32 [128, 2048, 512], P('grp', 'dev')
- shrinkage: float32 [128, 2048, 512], P('grp', 'dev')
- pressure: float32 [128, 2048, 512], P('grp', 'dev')
The draws below stay inside these ranges and needn't reach their ends.
Inputs may be any that keep to these rules, and one draw needn't show every extreme that they name: `tile_count`: the 4 bricks that share a second index together list exactly 32 tiles, and one of them lists 16. `tile_list`: the entries of one row are different. Pairs are mutual: if neighbours[a, 2k+1] = b then neighbours[b, 2k] = a, and the reverse. A slot s lies on device s // 8 = g * 32 + d; every neighbour of it lies on a device whose g // 2 and d // 2 equal those of s's device.
All inputs are finite; a program needn't handle non-finite values.
Results may differ from the reference program's by a relative error of at most 0.00002.
Values sent between devices are 32-bit elements; how exact they have to be, the bound alone decides.
A program may use at most 192 MiB of HBM per device.

```python
import math
import jax
import jax.numpy as jnp
from jax import lax

BX = 32
BY = 64
BZ = 512
TILES_SOLVER = 8
TILE = 16
STEPS = 2
SWEEPS = 4
TILES_BRICK = 256
LIST_MAX = 16
SLOTS = 1024
NX = 128
NY = 2048
NZ = 512
N_GRP = 4
N_DEV = 32


def draw_tile_count(key, part):
    key = jax.random.fold_in(key, 11)
    key_list = jax.random.split(key, N_DEV)
    others_n = N_GRP - 1
    total = (N_GRP - 2) * TILES_SOLVER

    def column(column_key):
        key_cut, key_top = jax.random.split(column_key)
        cut_points = jnp.sort(jax.random.permutation(key_cut, total - 1)[:others_n - 1] + 1).astype(jnp.int32)
        bounds = jnp.concatenate([jnp.zeros((1,), jnp.int32), cut_points, jnp.full((1,), total, jnp.int32)])
        others = bounds[1:] - bounds[:-1]
        busiest = jax.random.randint(key_top, (), 0, N_GRP)
        brick_idx = jnp.arange(N_GRP, dtype=jnp.int32)
        source_idx = jnp.clip(brick_idx - (brick_idx > busiest).astype(jnp.int32), 0, others_n - 1)
        return jnp.where(brick_idx == busiest, 2 * TILES_SOLVER, others[source_idx]).astype(jnp.int32)
    columns = jax.vmap(column)(key_list)
    return columns.T.reshape(-1).astype(jnp.int32)


def draw_tile_list(key, part):
    key = jax.random.fold_in(key, 12)
    key_list = jax.random.split(key, N_GRP * N_DEV)

    def one_row(row_key):
        return jax.random.permutation(row_key, TILES_BRICK)[:LIST_MAX].astype(jnp.int32)
    return jax.vmap(one_row)(key_list)


def draw_neighbours(key, part):
    key = jax.random.fold_in(key, 13)
    block_rows = N_GRP // 2
    block_cols = N_DEV // 2
    block_count = block_rows * block_cols
    per_block = 4 * TILES_SOLVER
    block_ids = jnp.arange(block_count, dtype=jnp.int32)
    local_q = jnp.arange(per_block, dtype=jnp.int32)
    grp_of = 2 * (block_ids // block_cols)[:, None] + (local_q // (2 * TILES_SOLVER))[None, :]
    dev_of = 2 * (block_ids % block_cols)[:, None] + (local_q // TILES_SOLVER % 2)[None, :]
    global_tab = ((grp_of * N_DEV + dev_of) * TILES_SOLVER + (local_q % TILES_SOLVER)[None, :]).astype(jnp.int32)
    columns = []
    for dim_no in range(3):
        key_pair, key_keep = jax.random.split(jax.random.fold_in(key, dim_no))
        perms = jax.vmap(lambda one_key: jax.random.permutation(one_key, per_block))(jax.random.split(key_pair, block_count)).astype(jnp.int32)
        kept_mask = jax.random.randint(key_keep, (block_count, per_block), 0, 4) > 0
        partner = jnp.take_along_axis(global_tab, perms, axis=1)
        upper_vals = jnp.where(kept_mask, partner, -1).astype(jnp.int32)
        lower_vals = jnp.where(kept_mask, global_tab, -1).astype(jnp.int32)
        upper_nbr = jnp.zeros((SLOTS,), jnp.int32).at[global_tab.reshape(-1)].set(upper_vals.reshape(-1))
        lower_nbr = jnp.zeros((SLOTS,), jnp.int32).at[partner.reshape(-1)].set(lower_vals.reshape(-1))
        columns.append(lower_nbr)
        columns.append(upper_nbr)
    return jnp.stack(columns, 1).astype(jnp.int32)


def shard_levels(own_key, dims, cuts, least, largest):
    def one(position, shards_of):
        heights = jax.random.uniform(jax.random.fold_in(jax.random.fold_in(own_key, 6), position), (shards_of,), jnp.float32, least / len(cuts), largest / len(cuts))
        return jnp.repeat(jnp.exp(heights), dims[position] // shards_of).reshape((-1,) + (1,) * (len(dims) - position - 1))

    gain = one(*cuts[0])
    for cut in cuts[1:]:
        gain = gain * one(*cut)
    return gain


def setup_inputs(seed: int = 0) -> dict:
    key_of = jax.random.split(jax.random.key(seed), 6)
    return {
        "enthalpy": jnp.clip(-0.5 + 2.0 * jax.random.uniform(key_of[0], (NX, NY, NZ), jnp.float32) ** shard_levels(key_of[0], (NX, NY, NZ), ((0, 4), (1, 32)), -0.2, 0.2), -0.5, 1.5),
        "conduct": jnp.clip(jnp.exp(math.log(1.0) - 2.3025851 * jax.random.uniform(key_of[1], (NX, NY, NZ), jnp.float32) ** shard_levels(key_of[1], (NX, NY, NZ), ((0, 4), (1, 32)), -0.2, 0.2)), 0.1, 1.0),
        "tile_count": draw_tile_count(jax.random.fold_in(key_of[5], 71), 0),
        "tile_list": draw_tile_list(jax.random.fold_in(key_of[5], 71), 0),
        "neighbours": draw_neighbours(jax.random.fold_in(key_of[5], 71), 0),
    }


heat_step = 0.15
base_perm = 0.5
perm_floor = 0.05
storage = 1.0
directions = ((-1, 0, 0), (1, 0, 0), (0, -1, 0), (0, 1, 0), (0, 0, -1), (0, 0, 1))


def shifted(source_array, offset):
    for dim_pos in range(3):
        dim_at = source_array.ndim - 3 + dim_pos
        source_array = lax.slice_in_dim(source_array, 1 + offset[dim_pos], source_array.shape[dim_at] - 1 + offset[dim_pos], axis=dim_at)
    return source_array


def thermal_step(h_padded, k_padded):
    liquid = jnp.clip(h_padded, 0.0, 1.0)
    temper = jnp.pad(h_padded - liquid, ((0, 0), (0, 0), (1, 1)))
    k_zpad = jnp.pad(k_padded, ((0, 0), (0, 0), (1, 1)))
    centre_t = shifted(temper, (0, 0, 0))
    centre_k = shifted(k_zpad, (0, 0, 0))
    flux_sum = jnp.zeros_like(centre_t)
    for direction in directions:
        face_k = 0.5 * (centre_k + shifted(k_zpad, direction))
        flux_sum = flux_sum + face_k * (shifted(temper, direction) - centre_t)
    return h_padded[1:-1, 1:-1, :] + heat_step * flux_sum


def permeability(liquid):
    return base_perm * liquid * liquid * liquid / ((1.0 - liquid) * (1.0 - liquid) + perm_floor)


def sweep(k_padded, p_padded, source):
    centre_k = shifted(k_padded, (0, 0, 0))
    inflow = jnp.zeros_like(source)
    diag_sum = jnp.zeros_like(source)
    for direction in directions:
        face_k = 0.5 * (centre_k + shifted(k_padded, direction))
        inflow = inflow + face_k * shifted(p_padded, direction)
        diag_sum = diag_sum + face_k
    return (source + inflow) / (storage + diag_sum)


def tile_faces(tile_set):
    count_t = tile_set.shape[0]
    face_set = jnp.stack([tile_set[:, 0], tile_set[:, -1], tile_set[:, :, 0], tile_set[:, :, -1], tile_set[:, :, :, 0], tile_set[:, :, :, -1]], 1)
    return face_set.reshape(count_t, 6, TILE * TILE)


def pick_ghosts(all_faces, neighbour_ids):
    opposite = jnp.array([1, 0, 3, 2, 5, 4], dtype=jnp.int32)
    picked = all_faces[jnp.maximum(neighbour_ids, 0), opposite[None, :]]
    return jnp.where((neighbour_ids >= 0)[..., None], picked, 0.0)


def with_ghosts(tile_set, ghosts):
    count_t = tile_set.shape[0]
    ghost_set = ghosts.reshape(count_t, 6, TILE, TILE)
    padded = jnp.pad(tile_set, ((0, 0), (1, 1), (1, 1), (1, 1)))
    padded = padded.at[:, 0, 1:-1, 1:-1].set(ghost_set[:, 0]).at[:, -1, 1:-1, 1:-1].set(ghost_set[:, 1])
    padded = padded.at[:, 1:-1, 0, 1:-1].set(ghost_set[:, 2]).at[:, 1:-1, -1, 1:-1].set(ghost_set[:, 3])
    padded = padded.at[:, 1:-1, 1:-1, 0].set(ghost_set[:, 4]).at[:, 1:-1, 1:-1, -1].set(ghost_set[:, 5])
    return padded


def to_tiles(field_in):
    size_x, size_y, size_z = field_in.shape
    blocks = field_in.reshape(size_x // TILE, TILE, size_y // TILE, TILE, size_z // TILE, TILE)
    return blocks.transpose(0, 2, 4, 1, 3, 5).reshape(-1, TILE * TILE * TILE)


def from_tiles(tile_set, shape):
    size_x, size_y, size_z = shape
    blocks = tile_set.reshape(size_x // TILE, size_y // TILE, size_z // TILE, TILE, TILE, TILE)
    return blocks.transpose(0, 3, 1, 4, 2, 5).reshape(size_x, size_y, size_z)


def to_bricks(field_in):
    return field_in.reshape(N_GRP, BX, N_DEV, BY, BZ).transpose(0, 2, 1, 3, 4).reshape(N_GRP * N_DEV, BX, BY, BZ)


def from_bricks(brick_set):
    return brick_set.reshape(N_GRP, N_DEV, BX, BY, BZ).transpose(0, 2, 1, 3, 4).reshape(N_GRP * BX, N_DEV * BY, BZ)


def reference(enthalpy, conduct, tile_count, tile_list, neighbours):
    k_padded = jnp.pad(conduct, ((1, 1), (1, 1), (0, 0)))
    current = enthalpy
    for step_no in range(STEPS):
        current = thermal_step(jnp.pad(current, ((1, 1), (1, 1), (0, 0))), k_padded)
    liquid_old = jnp.clip(enthalpy, 0.0, 1.0)
    liquid_new = jnp.clip(current, 0.0, 1.0)
    shrinkage = (liquid_old - liquid_new) / (STEPS * heat_step)
    darcy_perm = permeability(liquid_new)
    brick_count = N_GRP * N_DEV
    cells = TILE * TILE * TILE
    perm_tiles = jax.vmap(to_tiles)(to_bricks(darcy_perm))
    src_tiles = jax.vmap(to_tiles)(to_bricks(shrinkage))
    counts_grid = tile_count.reshape(N_GRP, N_DEV)
    offsets = (jnp.cumsum(counts_grid, axis=0) - counts_grid).astype(jnp.int32).reshape(-1)
    listing = jnp.arange(LIST_MAX, dtype=jnp.int32)
    column_pos = offsets[:, None] + listing[None, :]
    dev_col = (jnp.arange(brick_count, dtype=jnp.int32) % N_DEV)[:, None]
    solver_grp = (column_pos // TILES_SOLVER + N_GRP // 2) % N_GRP
    slot_ids = (solver_grp * N_DEV + dev_col) * TILES_SOLVER + column_pos % TILES_SOLVER
    is_valid = listing[None, :] < tile_count[:, None]
    slot_ids = jnp.where(is_valid, slot_ids, SLOTS).astype(jnp.int32)
    listed_perm = jnp.take_along_axis(perm_tiles, tile_list[:, :, None], axis=1).reshape(-1, cells)
    listed_src = jnp.take_along_axis(src_tiles, tile_list[:, :, None], axis=1).reshape(-1, cells)
    flat_ids = slot_ids.reshape(-1)
    solver_perm = jnp.zeros((SLOTS, cells), jnp.float32).at[flat_ids].set(listed_perm, mode="drop")
    solver_source = jnp.zeros((SLOTS, cells), jnp.float32).at[flat_ids].set(listed_src, mode="drop")
    solver_perm = solver_perm.reshape(SLOTS, TILE, TILE, TILE)
    solver_source = solver_source.reshape(SLOTS, TILE, TILE, TILE)
    k_tiles = with_ghosts(solver_perm, pick_ghosts(tile_faces(solver_perm), neighbours))
    solver_pressure = sweep(k_tiles, jnp.zeros_like(k_tiles), solver_source)
    for sweep_no in range(1, SWEEPS):
        ghosts = pick_ghosts(tile_faces(solver_pressure), neighbours)
        solver_pressure = sweep(k_tiles, with_ghosts(solver_pressure, ghosts), solver_source)
    flat_pressure = solver_pressure.reshape(SLOTS, cells)
    values = flat_pressure[jnp.clip(slot_ids, 0, SLOTS - 1)]
    target = jnp.where(is_valid, tile_list, TILES_BRICK).astype(jnp.int32)
    brick_rows = jnp.broadcast_to(jnp.arange(brick_count, dtype=jnp.int32)[:, None], target.shape)
    pressure_tiles = jnp.zeros((brick_count, TILES_BRICK, cells), jnp.float32).at[brick_rows, target].set(values, mode="drop")
    pressure_bricks = jax.vmap(lambda tile_set: from_tiles(tile_set, (BX, BY, BZ)))(pressure_tiles)
    return current, shrinkage, from_bricks(pressure_bricks)
```

```python
import functools

import jax
import jax.numpy as jnp
from jax import lax
from jax.experimental import pallas as pl
from jax.experimental.pallas import tpu as pltpu
from jax.sharding import PartitionSpec as P

MESH = pl.DeviceIdType.MESH
F32 = jnp.float32
BX, BY, BZ = 32, 64, 512
NZT = BZ // 128
YT = BY // 8
HEAT = 0.15
FLUX = 0.5 * HEAT
RATE = 1.0 / (2 * HEAT)
LISTED = 16
Y0 = 8
YP = BY + 2 * Y0


def clip01(v):
    return jnp.minimum(jnp.maximum(v, 0.0), 1.0)


def temper(v):
    return v - clip01(v)


def lanes():
    return lax.broadcasted_iota(jnp.int32, (8, 128), 1)


def up_z(row, end):
    first = lanes() == 127
    rolled = [pltpu.roll(v, 127, 1) for v in row]
    return [jnp.where(first, rolled[j + 1] if j + 1 < len(row) else end, rolled[j]) for j in range(len(row))]


def down_z(row, before):
    last = lanes() == 0
    rolled = [pltpu.roll(v, 1, 1) for v in row]
    return [jnp.where(last, rolled[j - 1] if j else before, rolled[j]) for j in range(len(row))]


def flux_row(t_ref, k_ref, kz_ref, x, yt, first):
    xp = x + 1
    lo = Y0 + 8 * yt
    mid = pl.ds(lo, 8)
    zts = range(NZT)
    t = [t_ref[xp, j, mid, :] for j in zts]
    k = [k_ref[xp, j, mid, :] for j in zts]
    tz = up_z(t, 0.0)
    if first:
        kup = up_z(k, 0.0)
        kz = [k[j] + kup[j] for j in zts]
        for j in zts:
            kz_ref[x, j, yt] = kz[j]
    else:
        kz = [kz_ref[x, j, yt] for j in zts]
    fz = [kz[j] * (tz[j] - t[j]) for j in zts]
    fzm = down_z(fz, k[0] * t[0])
    out = []
    for j in zts:
        acc = fz[j] - fzm[j]
        for dx, dy in ((1, 0), (-1, 0), (0, 1), (0, -1)):
            rows = pl.ds(lo + dy, 8)
            acc = acc + (k[j] + k_ref[xp + dx, j, rows, :]) * (t_ref[xp + dx, j, rows, :] - t[j])
        out.append(acc)
    return out


def first_rows(refs, x, yts):
    h0, h1, kp, t0, t1, kz = refs
    for yt in yts:
        acc = flux_row(t0, kp, kz, x, yt, True)
        for j in range(NZT):
            new = h0[x, j, yt] + FLUX * acc[j]
            h1[x, j, yt] = new
            t1[x + 1, j, pl.ds(Y0 + 8 * yt, 8), :] = temper(new)


def second_rows(refs, x, yts):
    h0, h1, kp, t0, t1, kz = refs
    for yt in yts:
        acc = flux_row(t1, kp, kz, x, yt, False)
        for j in range(NZT):
            new = h1[x, j, yt] + FLUX * acc[j]
            h1[x, j, yt] = new
            h0[x, j, yt] = (clip01(h0[x, j, yt]) - clip01(new)) * RATE


def over_planes(low, high, step, body):
    def one(i, carry):
        body(i)
        return carry

    lax.fori_loop(low, high, one, 0)


def cut_list(src, tl_ref, put):
    block = lanes() // 16

    def part(n, carry):
        group, half = n // 2, n % 2
        places = []
        for j in range(8):
            t = tl_ref[0, group * 8 + j]
            x0 = (t >> 7) * 16 + half * 8
            y0 = ((t >> 5) & 3) * 2
            up = (j - jnp.full((8, 128), t, jnp.int32)) & 7
            places.append((x0, y0, (t & 31) >> 3, [((up >> bit) & 1).astype(F32) for bit in range(3)]))
        rows = []
        for x in range(8):
            for yy in range(2):
                acc = jnp.zeros((8, 128), F32)
                for j, (x0, y0, zt, bits) in enumerate(places):
                    v = src[x0 + x, zt, y0 + yy]
                    for n_bit, bit in enumerate(bits):
                        v = bit * pltpu.roll(v, 16 << n_bit, 1) + (1.0 - bit) * v
                    acc = jnp.where(block == j, v, acc)
                rows.append(clip01(acc))
        put(half, group, jnp.concatenate(rows, axis=0).T)
        return carry

    lax.fori_loop(0, 4, part, 0)


def heat_kernel(
    h_ref, k_ref, tc_ref, tl_ref, nb_ref,
    h_out, s_out, old_out, new_out, nb_out,
    h0, h1, kp, t0, t1, kz, hx, kx, ysend, yrecv, y2send, y2recv, load_sem, send_sem, recv_sem,
):
    g, d = lax.axis_index("grp"), lax.axis_index("dev")
    n_g, n_d = lax.axis_size("grp"), lax.axis_size("dev")
    core = d % 2
    mate = d + 1 - 2 * core
    right, left = (g + 1) % n_g, (g + n_g - 1) % n_g
    above, below = (d + 1) % n_d, (d + n_d - 1) % n_d
    aside = (d + n_d + 2 * core - 1) % n_d

    loads = []
    for j in range(NZT):
        z = pl.ds(128 * j, 128)
        loads.append(pltpu.make_async_copy(h_ref.at[:, :, :, z], h0.at[:, j], load_sem.at[j]))
        loads.append(pltpu.make_async_copy(k_ref.at[:, :, z], kp.at[pl.ds(1, BX), j, pl.ds(Y0, BY), :], load_sem.at[NZT + j]))
    for copy in loads:
        copy.start()

    barrier = pltpu.get_barrier_semaphore()
    pair = [((g + dg) % n_g, mate if dc else d) for dg in range(4) for dc in range(2) if dg or dc]
    for peer in pair + [(g, aside)]:
        pl.semaphore_signal(barrier, inc=1, device_id=peer, device_id_type=MESH)
    pl.semaphore_wait(barrier, 8)

    def remote(n, src, dst, peer):
        return pltpu.make_async_remote_copy(
            src_ref=src, dst_ref=dst, send_sem=send_sem.at[n], recv_sem=recv_sem.at[n], device_id=peer, device_id_type=MESH
        )

    faces = [
        remote(0, h_ref.at[0], hx.at[1], (left, d)),
        remote(1, h_ref.at[BX - 1], hx.at[0], (right, d)),
        remote(2, k_ref.at[0], kx.at[1], (left, d)),
        remote(3, k_ref.at[BX - 1], kx.at[0], (right, d)),
    ]
    for copy in faces:
        copy.start()

    column = lax.broadcasted_iota(jnp.int32, (8, 128), 1)
    mine = nb_out.at[core * 4 + g]
    nb_out[core * 4 + g] = jnp.where(column == 6, tc_ref[0], jnp.zeros((8, 128), jnp.int32))
    nb_out[core * 4 + g, :, 0:6] = nb_ref[...]
    tables = [remote(10 + n, mine, mine, peer) for n, peer in enumerate(pair)]
    for copy in tables:
        copy.start()

    for copy in loads:
        copy.wait()

    def pack(x):
        for j in range(NZT):
            for side, row in ((0, 0), (1, BY - 1)):
                ysend[side, x, pl.ds(j, 1), :] = h0[x, j, row // 8, pl.ds(row % 8, 1), :]
                ysend[side, x, pl.ds(NZT + j, 1), :] = kp[x + 1, j, pl.ds(Y0 + row, 1), :]

    over_planes(0, BX, 1, pack)
    edges = [remote(4, ysend.at[0], yrecv.at[1], (g, below)), remote(5, ysend.at[1], yrecv.at[0], (g, above))]
    for copy in edges:
        copy.start()

    def ring(base, buf):
        own = buf.at[core, g]
        from_left, from_right, far = buf.at[core, left], buf.at[core, right], buf.at[core, (g + 2) % n_g]
        return dict(
            first=[
                remote(base + 0, own.at[0], own.at[0], (right, d)),
                remote(base + 1, own.at[1], own.at[1], (left, d)),
                remote(base + 2, own.at[1], own.at[1], (right, d)),
                remote(base + 3, own.at[0], own.at[0], (left, d)),
            ],
            onward=[
                remote(base + 4, from_left.at[0], from_left.at[0], (right, d)),
                remote(base + 5, from_right.at[1], from_right.at[1], (left, d)),
            ],
            mate=[
                remote(base + 6, own, own, (g, mate)),
                remote(base + 7, from_left.at[0], from_left.at[0], (g, mate)),
                remote(base + 8, from_right.at[1], from_right.at[1], (g, mate)),
                remote(base + 9, from_left.at[1], from_left.at[1], (g, mate)),
                remote(base + 10, from_right.at[0], from_right.at[0], (g, mate)),
                remote(base + 11, far.at[0], far.at[0], (g, mate)),
                remote(base + 12, far.at[1], far.at[1], (g, mate)),
            ],
        )

    def ring_open(r):
        for copy in r["first"]:
            copy.start()
        r["mate"][0].start()

    def ring_pass(r):
        r["first"][0].wait_recv()
        r["onward"][0].start()
        r["mate"][1].start()
        r["first"][1].wait_recv()
        r["onward"][1].start()
        r["mate"][2].start()

    def ring_close(r):
        r["first"][2].wait_recv()
        r["mate"][3].start()
        r["first"][3].wait_recv()
        r["mate"][4].start()
        r["onward"][0].wait_recv()
        r["mate"][5].start()
        r["onward"][1].wait_recv()
        r["mate"][6].start()
        for copy in r["mate"]:
            copy.wait_recv()
        for copy in r["first"] + r["onward"] + r["mate"]:
            copy.wait_send()

    def put_into(buf):
        def put(half, group, value):
            buf[core, g, half, pl.ds(pl.multiple_of(group * 128, 128), 128), :] = value

        return put

    old_ring, new_ring = ring(20, old_out), ring(40, new_out)
    cut_list(h0, tl_ref, put_into(old_out))
    ring_open(old_ring)

    refs = (h0, h1, kp, t0, t1, kz)

    def warm(x):
        for j in range(NZT):
            for yt in range(YT):
                t0[x + 1, j, pl.ds(Y0 + 8 * yt, 8), :] = temper(h0[x, j, yt])

    over_planes(0, BX, 1, warm)
    inner, rim = range(1, YT - 1), (0, YT - 1)
    over_planes(1, BX - 1, 1, lambda x: first_rows(refs, x, inner))

    for copy in edges:
        copy.wait_recv()

    def unpack(x):
        for j in range(NZT):
            for side, row, real in ((0, Y0 - 1, d > 0), (1, Y0 + BY, d < n_d - 1)):
                t0[x + 1, j, pl.ds(row, 1), :] = jnp.where(real, temper(yrecv[side, x, pl.ds(j, 1), :]), 0.0)
                kp[x + 1, j, pl.ds(row, 1), :] = jnp.where(real, yrecv[side, x, pl.ds(NZT + j, 1), :], 0.0)

    over_planes(0, BX, 1, unpack)
    over_planes(1, BX - 1, 1, lambda x: first_rows(refs, x, rim))

    for copy in faces:
        copy.wait_recv()
    for side, plane, real in ((0, 0, g > 0), (1, BX + 1, g < n_g - 1)):
        for j in range(NZT):
            z = pl.ds(128 * j, 128)
            for yt in range(YT):
                rows = pl.ds(8 * yt, 8)
                t0[plane, j, pl.ds(Y0 + 8 * yt, 8), :] = jnp.where(real, temper(hx[side, yt, :, z]), 0.0)
                kp[plane, j, pl.ds(Y0 + 8 * yt, 8), :] = jnp.where(real, kx[side, rows, z], 0.0)
    for x in (0, BX - 1):
        first_rows(refs, x, range(YT))

    inside = pl.ds(Y0, BY)
    faces2 = [
        remote(6, t1.at[1, :, inside, :], t1.at[BX + 1, :, inside, :], (left, d)),
        remote(7, t1.at[BX, :, inside, :], t1.at[0, :, inside, :], (right, d)),
    ]
    for copy in faces2:
        copy.start()

    def pack2(x):
        for odd in range(2):
            for j in range(NZT):
                for side, row in ((0, Y0), (1, Y0 + BY - 1)):
                    y2send[side, x, pl.ds(odd * NZT + j, 1), :] = t1[2 * x + odd + 1, j, pl.ds(row, 1), :]

    over_planes(0, BX // 2, 1, pack2)
    edges2 = [remote(8, y2send.at[0], y2recv.at[1], (g, below)), remote(9, y2send.at[1], y2recv.at[0], (g, above))]
    for copy in edges2:
        copy.start()
    ring_pass(old_ring)

    over_planes(1, BX - 1, 1, lambda x: second_rows(refs, x, inner))
    for copy in edges2:
        copy.wait_recv()

    def unpack2(x):
        for odd in range(2):
            for j in range(NZT):
                for side, row, real in ((0, Y0 - 1, d > 0), (1, Y0 + BY, d < n_d - 1)):
                    t1[2 * x + odd + 1, j, pl.ds(row, 1), :] = jnp.where(
                        real, y2recv[side, x, pl.ds(odd * NZT + j, 1), :], 0.0
                    )

    over_planes(0, BX // 2, 1, unpack2)
    over_planes(1, BX - 1, 1, lambda x: second_rows(refs, x, rim))
    for copy in faces2:
        copy.wait()
    for plane, outside in ((0, g == 0), (BX + 1, g == n_g - 1)):

        @pl.when(outside)
        def _():
            for j in range(NZT):
                for yt in range(YT):
                    t1[plane, j, pl.ds(Y0 + 8 * yt, 8), :] = jnp.zeros((8, 128), F32)

    for x in (0, BX - 1):
        second_rows(refs, x, range(YT))

    cut_list(h1, tl_ref, put_into(new_out))
    ring_open(new_ring)
    stores = []
    for j in range(NZT):
        z = pl.ds(128 * j, 128)
        stores.append(pltpu.make_async_copy(h1.at[:, j], h_out.at[:, :, :, z], load_sem.at[j]))
        stores.append(pltpu.make_async_copy(h0.at[:, j], s_out.at[:, :, :, z], load_sem.at[NZT + j]))
    for copy in stores:
        copy.start()
    ring_close(old_ring)
    ring_pass(new_ring)
    ring_close(new_ring)
    for copy in stores:
        copy.wait()
    for copy in faces + edges + edges2:
        copy.wait_send()
    for copy in tables:
        copy.wait()


PZ = 10 * 32
PAD_ROWS = 18 * PZ
CUT = 80 * 16


def at_row(z, x, y):
    return (z + 1) * PZ + (x + 1) * 32 + y + 8


def permute(v, index, mask):
    return jnp.where(mask, jnp.take_along_axis(v, index, axis=1, mode="promise_in_bounds"), 0.0)


def ghosts(buf, index, mask):
    def plane(z, carry):
        for yy in range(2):
            for face, src, dst in ((0, 7, -1), (1, 0, 8)):
                v = buf[pl.ds(at_row(z, src, 8 * yy), 8), :]
                buf[pl.ds(at_row(z, dst, 8 * yy), 8), :] = permute(v, index[face], mask[face])
        for face, src, dst in ((2, 15, -1), (3, 0, 16)):
            v = buf[pl.ds(at_row(z, 0, src), 8, stride=32), :]
            buf[pl.ds(at_row(z, 0, dst), 8, stride=32), :] = permute(v, index[face], mask[face])
        return carry

    lax.fori_loop(0, 16, plane, 0)
    for x in range(8):
        for yy in range(2):
            for face, src, dst in ((4, 15, -1), (5, 0, 16)):
                v = buf[pl.ds(at_row(src, x, 8 * yy), 8), :]
                buf[pl.ds(at_row(dst, x, 8 * yy), 8), :] = permute(v, index[face], mask[face])


def solve_kernel(
    h_ref, s_ref, old_ref, new_ref, nbs_ref, nbv_ref, tl_ref,
    h_out, s_out, p_out,
    old_c, new_c, kb, pa, pb, src, dg, fx, fy, fz, back, tmp, unit, field, hs, ss, sem,
):
    g, d = lax.axis_index("grp"), lax.axis_index("dev")
    core = d % 2
    ins = [pltpu.make_async_copy(h_ref, hs, sem.at[0]), pltpu.make_async_copy(s_ref, ss, sem.at[1])]
    for copy in ins:
        copy.start()

    first = jnp.int32(0)
    for c in range(2):
        start = jnp.int32(0)
        for q in range(4):
            count = nbs_ref[c * 4 + q, 0, 6]

            def move(i, carry, c=c, q=q, start=start):
                to = pl.multiple_of((c * 32 + start + i) * 16, 16)
                at = pl.multiple_of(i * 16, 16)
                for half in range(2):
                    old_c[pl.ds(half * CUT + to, 16), :] = old_ref[c, q, half, pl.ds(at, 16), :]
                    new_c[pl.ds(half * CUT + to, 16), :] = new_ref[c, q, half, pl.ds(at, 16), :]
                return carry

            lax.fori_loop(0, count, move, 0)
            first = jnp.where((g == q) & (core == c), c * 32 + start, first)
            start = start + count

    def spread(z, carry):
        def turned(ref):
            halves = [ref[pl.ds(half * CUT + z, 64, stride=16), :] for half in range(2)]
            return jnp.concatenate(halves, axis=0).T

        old, new = turned(old_c), turned(new_c)
        rest = 1.0 - new
        perm = 0.5 * new * new * new / (rest * rest + 0.05)
        src[pl.ds(pl.multiple_of(z * 128, 128), 128), :] = (old - new) * RATE
        for x in range(8):
            kb[pl.ds(at_row(z, x, 0), 16), :] = perm[16 * x : 16 * x + 16, :]
        return carry

    lax.fori_loop(0, 16, spread, 0)

    order = [nbv_ref[c * 4 + (blk + 2) % 4] for c in range(2) for blk in range(4)]
    table = jnp.concatenate(order + order, axis=0).astype(F32).T.astype(jnp.int32)
    lane = lanes()
    lane_half, lane_q = lane // 64, lane % 64
    index, mask = [], []
    for face in range(6):
        n = jnp.broadcast_to(table[face : face + 1, :], (8, 128))
        real = n >= 0
        n = jnp.maximum(n, 0)
        owner = n // 8
        q = (owner % 2) * 32 + ((owner // 32 + 2) % 4) * 8 + n % 8
        if face == 0:
            q, real = jnp.where(lane_half == 1, lane_q, q + 64), (lane_half == 1) | real
        elif face == 1:
            q, real = jnp.where(lane_half == 0, lane_q + 64, q), (lane_half == 0) | real
        else:
            q = q + 64 * lane_half
        index.append(q)
        mask.append(real)

    outs = [pltpu.make_async_copy(hs, h_out, sem.at[0]), pltpu.make_async_copy(ss, s_out, sem.at[1])]
    for before, after in zip(ins, outs):
        before.wait()
        after.start()
    ghosts(kb, index, mask)

    def each(body):
        def plane(z, carry):
            for x in range(8):
                for yy in range(2):
                    body(z, x, yy)
            return carry

        lax.fori_loop(0, 16, plane, 0)

    def k_at(z, x, y):
        return kb[pl.ds(at_row(z, x, y), 8), :]

    def flat(z, x, yy, xs=8, ys=16):
        return pl.ds((z * xs + x) * ys + 8 * yy, 8)

    def coefficients(z, x, yy):
        mid = k_at(z, x, 8 * yy)
        up = 0.5 * (mid + k_at(z, x + 1, 8 * yy))
        fx[flat(z, x + 1, yy, 9), :] = up
        down = 0.5 * (mid + k_at(z, x - 1, 8 * yy))
        if x == 0:
            fx[flat(z, 0, yy, 9), :] = down
        yup = 0.5 * (mid + k_at(z, x, 8 * yy + 1))
        ydown = 0.5 * (mid + k_at(z, x, 8 * yy - 1))
        if yy == 0:
            fy[pl.ds((z * 8 + x) * 24, 8), :] = ydown
        fy[pl.ds((z * 8 + x) * 24 + 8 * yy + 1, 8), :] = yup
        zup = 0.5 * (mid + k_at(z + 1, x, 8 * yy))
        zdown = 0.5 * (mid + k_at(z - 1, x, 8 * yy))
        fz[flat(z + 1, x, yy), :] = zup
        fz[flat(z, x, yy), :] = zdown
        inverse = 1.0 / (1.0 + (down + up + ydown + yup + zdown + zup))
        dg[flat(z, x, yy), :] = inverse
        pa[pl.ds(at_row(z, x, 8 * yy), 8), :] = src[flat(z, x, yy), :] * inverse

    each(coefficients)

    def sweep(a, b):
        ghosts(a, index, mask)

        def cell(z, x, yy):
            def p(dz, dx, dy):
                return a[pl.ds(at_row(z + dz, x + dx, 8 * yy + dy), 8), :]

            total = src[flat(z, x, yy), :]
            total += fx[flat(z, x, yy, 9), :] * p(0, -1, 0) + fx[flat(z, x + 1, yy, 9), :] * p(0, 1, 0)
            low = (z * 8 + x) * 24 + 8 * yy
            total += fy[pl.ds(low, 8), :] * p(0, 0, -1) + fy[pl.ds(low + 1, 8), :] * p(0, 0, 1)
            total += fz[flat(z, x, yy), :] * p(-1, 0, 0) + fz[flat(z + 1, x, yy), :] * p(1, 0, 0)
            b[pl.ds(at_row(z, x, 8 * yy), 8), :] = total * dg[flat(z, x, yy), :]

        each(cell)

    sweep(pa, pb)
    sweep(pb, pa)
    sweep(pa, pb)

    def turn_back(z, carry):
        rows = [pb[pl.ds(at_row(z, x, 0), 16), :] for x in range(8)]
        back[pl.ds(pl.multiple_of(z * 144, 8), 128), :] = jnp.concatenate(rows, axis=0).T
        return carry

    lax.fori_loop(0, 16, turn_back, 0)

    def blank(x, carry):
        for j in range(NZT):
            field[x, j] = jnp.zeros((BY, 128), F32)
        return carry

    lax.fori_loop(0, BX, blank, 0)

    for group in range(2):
        for half in range(2):
            for z in range(16):
                v = back[pl.ds(z * 144 + half * 64 + first + group * 8, 8), :]
                tmp[pl.ds(z, 8, stride=16), :] = v
            unit[pl.ds((group * 2 + half) * 128, 128), :] = tmp[...].T

    block = lanes() // 16
    listed = nbs_ref[core * 4 + g, 0, 6]

    def place(i, carry):
        t = tl_ref[0, i]
        x0 = (t // 128) * 16
        y0 = pl.multiple_of(((t // 32) % 4) * 16, 16)
        tz = t % 32
        zt, slot = tz // 8, tz % 8
        shift = (slot * 16 - (i % 8) * 16 + 128) % 128
        for half in range(2):
            for x in range(8):
                for yy in range(2):
                    row = pl.multiple_of((i // 8 * 2 + half) * 128 + x * 16 + 8 * yy, 8)
                    v = pltpu.roll(unit[pl.ds(row, 8), :], shift, 1)
                    rows = pl.ds(y0 + 8 * yy, 8)
                    field[x0 + half * 8 + x, zt, rows, :] = jnp.where(block == slot, v, field[x0 + half * 8 + x, zt, rows, :])
        return carry

    lax.fori_loop(0, listed, place, 0)
    stores = [pltpu.make_async_copy(field.at[:, j], p_out.at[:, :, pl.ds(128 * j, 128)], sem.at[2 + j]) for j in range(NZT)]
    for copy in stores:
        copy.start()
    for copy in stores + outs:
        copy.wait()


VM = pl.BlockSpec(memory_space=pltpu.VMEM)
SM = pl.BlockSpec(memory_space=pltpu.SMEM)
ANY = pl.BlockSpec(memory_space=pl.ANY)


def solve_call(h_new, shrink, old_l, new_l, table, tile_list):
    brick = jax.ShapeDtypeStruct((BX, BY, BZ), F32)
    cells = (BX, NZT, BY, 128)
    return pl.pallas_call(
        solve_kernel,
        out_shape=[brick, brick, brick],
        in_specs=[ANY, ANY, VM, VM, SM, VM, SM],
        out_specs=[ANY, ANY, ANY],
        scratch_shapes=[
            pltpu.VMEM((2 * CUT, 128), F32),
            pltpu.VMEM((2 * CUT, 128), F32),
            pltpu.VMEM((PAD_ROWS, 128), F32),
            pltpu.VMEM((PAD_ROWS, 128), F32),
            pltpu.VMEM((PAD_ROWS, 128), F32),
            pltpu.VMEM((2048, 128), F32),
            pltpu.VMEM((2048, 128), F32),
            pltpu.VMEM((16 * 9 * 16, 128), F32),
            pltpu.VMEM((16 * 8 * 24, 128), F32),
            pltpu.VMEM((17 * 8 * 16, 128), F32),
            pltpu.VMEM((16 * 144, 128), F32),
            pltpu.VMEM((128, 128), F32),
            pltpu.VMEM((512, 128), F32),
            pltpu.VMEM(cells, F32),
            pltpu.VMEM((BX, BY, BZ), F32),
            pltpu.VMEM((BX, BY, BZ), F32),
            pltpu.SemaphoreType.DMA((2 + NZT,)),
        ],
        compiler_params=pltpu.CompilerParams(vmem_limit_bytes=50 * 2**20),
        cost_estimate=pl.CostEstimate(flops=20 * 2**20, bytes_accessed=40 * 2**20, transcendentals=0),
        name="solve_tiles",
    )(h_new, shrink, old_l, new_l, table, table, tile_list)


def local(enthalpy, conduct, tile_count, tile_list, neighbours):
    brick = jax.ShapeDtypeStruct((BX, YT, 8, BZ), F32)
    lists = jax.ShapeDtypeStruct((2, 4, 2, 256, 128), F32)
    cells = (BX, NZT, YT, 8, 128)
    padded = (BX + 2, NZT, YP, 128)
    h_new, shrink, old_l, new_l, table = pl.pallas_call(
        heat_kernel,
        out_shape=[brick, brick, lists, lists, jax.ShapeDtypeStruct((8, 8, 128), jnp.int32)],
        in_specs=[ANY, ANY, SM, SM, VM],
        out_specs=[ANY, ANY, VM, VM, VM],
        scratch_shapes=[
            pltpu.VMEM(cells, F32),
            pltpu.VMEM(cells, F32),
            pltpu.VMEM(padded, F32),
            pltpu.VMEM(padded, F32),
            pltpu.VMEM(padded, F32),
            pltpu.VMEM(cells, F32),
            pltpu.VMEM((2, YT, 8, BZ), F32),
            pltpu.VMEM((2, BY, BZ), F32),
            pltpu.VMEM((2, BX, 2 * NZT, 128), F32),
            pltpu.VMEM((2, BX, 2 * NZT, 128), F32),
            pltpu.VMEM((2, BX // 2, 2 * NZT, 128), F32),
            pltpu.VMEM((2, BX // 2, 2 * NZT, 128), F32),
            pltpu.SemaphoreType.DMA((2 * NZT,)),
            pltpu.SemaphoreType.DMA((60,)),
            pltpu.SemaphoreType.DMA((60,)),
        ],
        compiler_params=pltpu.CompilerParams(collective_id=0, has_side_effects=True, vmem_limit_bytes=50 * 2**20),
        cost_estimate=pl.CostEstimate(flops=80 * BX * BY * BZ, bytes_accessed=20 * 2**20, transcendentals=0),
        name="heat_steps",
    )(enthalpy.reshape(BX, YT, 8, BZ), conduct, tile_count, tile_list, neighbours)
    return solve_call(h_new.reshape(BX, BY, BZ), shrink.reshape(BX, BY, BZ), old_l, new_l, table, tile_list)


def solution(mesh):
    placed = (
        P("grp", "dev", None),
        P("grp", "dev", None),
        P(("grp", "dev")),
        P(("grp", "dev"), None),
        P(("grp", "dev"), None),
    )
    return jax.shard_map(
        local,
        mesh=mesh,
        in_specs=placed,
        out_specs=(P("grp", "dev", None), P("grp", "dev", None), P("grp", "dev", None)),
        check_vma=False,
    )
```

```python
import functools

import jax
import jax.numpy as jnp
from jax import lax
from jax.experimental import pallas as pl
from jax.experimental.pallas import tpu as pltpu
from jax.sharding import PartitionSpec as P

MESH = pl.DeviceIdType.MESH
F32 = jnp.float32
BX, BY, BZ = 32, 64, 512
NZT = BZ // 128
YT = BY // 8
HEAT = 0.15
FLUX = 0.5 * HEAT
RATE = 1.0 / (2 * HEAT)
LISTED = 16
Y0 = 8
YP = BY + 2 * Y0


def clip01(v):
    return jnp.minimum(jnp.maximum(v, 0.0), 1.0)


def temper(v):
    return v - clip01(v)


def lanes():
    return lax.broadcasted_iota(jnp.int32, (8, 128), 1)


def up_z(row, end):
    first = lanes() == 127
    rolled = [pltpu.roll(v, 127, 1) for v in row]
    return [jnp.where(first, rolled[j + 1] if j + 1 < len(row) else end, rolled[j]) for j in range(len(row))]


def down_z(row, before):
    last = lanes() == 0
    rolled = [pltpu.roll(v, 1, 1) for v in row]
    return [jnp.where(last, rolled[j - 1] if j else before, rolled[j]) for j in range(len(row))]


def flux_row(t_ref, k_ref, kz_ref, x, yt):
    xp = x + 1
    lo = Y0 + 8 * yt
    mid = pl.ds(lo, 8)
    zts = range(NZT)
    t = [t_ref[xp, j, mid, :] for j in zts]
    k = [k_ref[xp, j, mid, :] for j in zts]
    tz = up_z(t, 0.0)
    kz = [kz_ref[x, j, yt] for j in zts]
    fz = [kz[j] * (tz[j] - t[j]) for j in zts]
    fzm = down_z(fz, k[0] * t[0])
    out = []
    for j in zts:
        acc = fz[j] - fzm[j]
        for dx, dy in ((1, 0), (-1, 0), (0, 1), (0, -1)):
            rows = pl.ds(lo + dy, 8)
            acc = acc + (k[j] + k_ref[xp + dx, j, rows, :]) * (t_ref[xp + dx, j, rows, :] - t[j])
        out.append(acc)
    return out


def finish(refs, x, yt, acc, first):
    h0, h1, kp, t0, t1, kz, fx = refs
    for j in range(NZT):
        if first:
            new = h0[x, j, yt] + FLUX * acc[j]
            t1[x + 1, j, pl.ds(Y0 + 8 * yt, 8), :] = temper(new)
        else:
            new = h1[x, j, yt] + FLUX * acc[j]
            h0[x, j, yt] = (clip01(h0[x, j, yt]) - clip01(new)) * RATE
        h1[x, j, yt] = new


def outer_plane(refs, x, first):
    h0, h1, kp, t0, t1, kz, fx = refs
    for yt in range(YT):
        finish(refs, x, yt, flux_row(t0 if first else t1, kp, kz, x, yt), first)


def face_flux(refs, x, first):
    h0, h1, kp, t0, t1, kz, fx = refs
    t_ref = t0 if first else t1
    for yt in range(YT):
        rows = pl.ds(Y0 + 8 * yt, 8)
        for j in range(NZT):
            fx[j, yt] = (kp[x, j, rows, :] + kp[x + 1, j, rows, :]) * (t_ref[x + 1, j, rows, :] - t_ref[x, j, rows, :])


def plane_pair(refs, x, yts, first):
    h0, h1, kp, t0, t1, kz, fx = refs
    t_ref = t0 if first else t1
    zts = range(NZT)
    for yt in yts:
        lo = Y0 + 8 * yt
        rows = pl.ds(lo, 8)
        t = [[t_ref[x + 1 + p, j, rows, :] for j in zts] for p in range(3)]
        k = [[kp[x + 1 + p, j, rows, :] for j in zts] for p in range(3)]
        face = [[fx[j, yt] for j in zts]]
        for p in range(2):
            face.append([(k[p][j] + k[p + 1][j]) * (t[p + 1][j] - t[p][j]) for j in zts])
        for j in zts:
            fx[j, yt] = face[2][j]
        for p in range(2):
            xp = x + p
            acc = [face[p + 1][j] - face[p][j] for j in zts]
            for dy in (1, -1):
                side = pl.ds(lo + dy, 8)
                acc = [acc[j] + (k[p][j] + kp[xp + 1, j, side, :]) * (t_ref[xp + 1, j, side, :] - t[p][j]) for j in zts]
            tz = up_z(t[p], 0.0)
            kzs = [kz[xp, j, yt] for j in zts]
            fz = [kzs[j] * (tz[j] - t[p][j]) for j in zts]
            fzm = down_z(fz, k[p][0] * t[p][0])
            finish(refs, xp, yt, [acc[j] + (fz[j] - fzm[j]) for j in zts], first)


def over_planes(low, high, step, body):
    def one(i, carry):
        body(i)
        return carry

    lax.fori_loop(low, high, one, 0)


def cut_list(src, tl_ref, turned, put):
    def part(i, carry):
        t = tl_ref[0, i]
        x0, y0, zt, at = (t >> 7) * 16, ((t >> 5) & 3) * 2, (t & 31) >> 3, (t & 7) * 2
        for half in range(2):
            block = [src[x0 + half * 8 + x, zt, y0 + yy] for x in range(8) for yy in range(2)]
            turned[half] = clip01(jnp.concatenate(block, axis=0)).T.reshape(16, 8, 128)
            for q in range(2):
                put(half, i * 16 + q * 8, turned[half, at + q])
        return carry

    lax.fori_loop(0, LISTED, part, 0)


def heat_kernel(
    h_ref, k_ref, tc_ref, tl_ref, nb_ref,
    h_out, s_out, old_out, new_out, nb_out,
    h0, h1, kp, t0, t1, kz, fx, hx, kx, ysend, yrecv, y2send, y2recv, turned, load_sem, send_sem, recv_sem,
):
    g, d = lax.axis_index("grp"), lax.axis_index("dev")
    n_g, n_d = lax.axis_size("grp"), lax.axis_size("dev")
    core = d % 2
    mate = d + 1 - 2 * core
    right, left = (g + 1) % n_g, (g + n_g - 1) % n_g
    above, below = (d + 1) % n_d, (d + n_d - 1) % n_d
    aside = (d + n_d + 2 * core - 1) % n_d

    loads = []
    for j in range(NZT):
        z = pl.ds(128 * j, 128)
        loads.append(pltpu.make_async_copy(h_ref.at[:, :, :, z], h0.at[:, j], load_sem.at[j]))
        loads.append(pltpu.make_async_copy(k_ref.at[:, :, z], kp.at[pl.ds(1, BX), j, pl.ds(Y0, BY), :], load_sem.at[NZT + j]))
    for copy in loads:
        copy.start()

    barrier = pltpu.get_barrier_semaphore()
    pair = [((g + dg) % n_g, mate if dc else d) for dg in range(4) for dc in range(2) if dg or dc]
    for peer in pair + [(g, aside)]:
        pl.semaphore_signal(barrier, inc=1, device_id=peer, device_id_type=MESH)
    pl.semaphore_wait(barrier, 8)

    def remote(n, src, dst, peer):
        return pltpu.make_async_remote_copy(
            src_ref=src, dst_ref=dst, send_sem=send_sem.at[n], recv_sem=recv_sem.at[n], device_id=peer, device_id_type=MESH
        )

    faces = [
        remote(0, h_ref.at[0], hx.at[1], (left, d)),
        remote(1, h_ref.at[BX - 1], hx.at[0], (right, d)),
        remote(2, k_ref.at[0], kx.at[1], (left, d)),
        remote(3, k_ref.at[BX - 1], kx.at[0], (right, d)),
    ]
    for copy in faces:
        copy.start()

    column = lax.broadcasted_iota(jnp.int32, (8, 128), 1)
    mine = nb_out.at[core * 4 + g]
    nb_out[core * 4 + g] = jnp.where(column == 6, tc_ref[0], jnp.zeros((8, 128), jnp.int32))
    nb_out[core * 4 + g, :, 0:6] = nb_ref[...]
    tables = [remote(10 + n, mine, mine, peer) for n, peer in enumerate(pair)]
    for copy in tables:
        copy.start()

    for copy in loads:
        copy.wait()

    def pack(x):
        for j in range(NZT):
            for side, row in ((0, 0), (1, BY - 1)):
                ysend[side, x, pl.ds(j, 1), :] = h0[x, j, row // 8, pl.ds(row % 8, 1), :]
                ysend[side, x, pl.ds(NZT + j, 1), :] = kp[x + 1, j, pl.ds(Y0 + row, 1), :]

    over_planes(0, BX, 1, pack)
    edges = [remote(4, ysend.at[0], yrecv.at[1], (g, below)), remote(5, ysend.at[1], yrecv.at[0], (g, above))]
    for copy in edges:
        copy.start()

    def ring(base, buf):
        own = buf.at[core, g]
        from_left, from_right, far = buf.at[core, left], buf.at[core, right], buf.at[core, (g + 2) % n_g]
        return dict(
            first=[
                remote(base + 0, own.at[0], own.at[0], (right, d)),
                remote(base + 1, own.at[1], own.at[1], (left, d)),
                remote(base + 2, own.at[1], own.at[1], (right, d)),
                remote(base + 3, own.at[0], own.at[0], (left, d)),
            ],
            onward=[
                remote(base + 4, from_left.at[0], from_left.at[0], (right, d)),
                remote(base + 5, from_right.at[1], from_right.at[1], (left, d)),
            ],
            mate=[
                remote(base + 6, own, own, (g, mate)),
                remote(base + 7, from_left.at[0], from_left.at[0], (g, mate)),
                remote(base + 8, from_right.at[1], from_right.at[1], (g, mate)),
                remote(base + 9, from_left.at[1], from_left.at[1], (g, mate)),
                remote(base + 10, from_right.at[0], from_right.at[0], (g, mate)),
                remote(base + 11, far.at[0], far.at[0], (g, mate)),
                remote(base + 12, far.at[1], far.at[1], (g, mate)),
            ],
        )

    def ring_open(r):
        for copy in r["first"]:
            copy.start()
        r["mate"][0].start()

    def ring_pass(r):
        r["first"][0].wait_recv()
        r["onward"][0].start()
        r["mate"][1].start()
        r["first"][1].wait_recv()
        r["onward"][1].start()
        r["mate"][2].start()

    def ring_close(r):
        r["first"][2].wait_recv()
        r["mate"][3].start()
        r["first"][3].wait_recv()
        r["mate"][4].start()
        r["onward"][0].wait_recv()
        r["mate"][5].start()
        r["onward"][1].wait_recv()
        r["mate"][6].start()
        for copy in r["mate"]:
            copy.wait_recv()
        for copy in r["first"] + r["onward"] + r["mate"]:
            copy.wait_send()

    def put_into(buf):
        def put(half, row, value):
            buf[core, g, half, pl.ds(pl.multiple_of(row, 8), 8), :] = value

        return put

    old_ring, new_ring = ring(20, old_out), ring(40, new_out)
    cut_list(h0, tl_ref, turned, put_into(old_out))
    ring_open(old_ring)

    refs = (h0, h1, kp, t0, t1, kz, fx)

    def warm(i):
        for x in range(4):
            for yt in range(YT):
                rows = pl.ds(Y0 + 8 * yt, 8)
                k = [kp[4 * i + x + 1, j, rows, :] for j in range(NZT)]
                above_k = up_z(k, 0.0)
                for j in range(NZT):
                    kz[4 * i + x, j, yt] = k[j] + above_k[j]
                    t0[4 * i + x + 1, j, rows, :] = temper(h0[4 * i + x, j, yt])

    over_planes(0, BX // 4, 1, warm)

    for copy in edges:
        copy.wait_recv()

    def unpack(x):
        for j in range(NZT):
            for side, row, real in ((0, Y0 - 1, d > 0), (1, Y0 + BY, d < n_d - 1)):
                t0[x + 1, j, pl.ds(row, 1), :] = jnp.where(real, temper(yrecv[side, x, pl.ds(j, 1), :]), 0.0)
                kp[x + 1, j, pl.ds(row, 1), :] = jnp.where(real, yrecv[side, x, pl.ds(NZT + j, 1), :], 0.0)

    over_planes(0, BX, 1, unpack)
    face_flux(refs, 1, True)
    over_planes(0, BX // 2 - 1, 1, lambda i: plane_pair(refs, 2 * i + 1, range(YT), True))

    for copy in faces:
        copy.wait_recv()
    for side, plane, real in ((0, 0, g > 0), (1, BX + 1, g < n_g - 1)):
        for j in range(NZT):
            z = pl.ds(128 * j, 128)
            for yt in range(YT):
                rows = pl.ds(8 * yt, 8)
                t0[plane, j, pl.ds(Y0 + 8 * yt, 8), :] = jnp.where(real, temper(hx[side, yt, :, z]), 0.0)
                kp[plane, j, pl.ds(Y0 + 8 * yt, 8), :] = jnp.where(real, kx[side, rows, z], 0.0)
    for x in (0, BX - 1):
        outer_plane(refs, x, True)

    inside = pl.ds(Y0, BY)
    faces2 = [
        remote(6, t1.at[1, :, inside, :], t1.at[BX + 1, :, inside, :], (left, d)),
        remote(7, t1.at[BX, :, inside, :], t1.at[0, :, inside, :], (right, d)),
    ]
    for copy in faces2:
        copy.start()

    def pack2(x):
        for odd in range(2):
            for j in range(NZT):
                for side, row in ((0, Y0), (1, Y0 + BY - 1)):
                    y2send[side, x, pl.ds(odd * NZT + j, 1), :] = t1[2 * x + odd + 1, j, pl.ds(row, 1), :]

    over_planes(0, BX // 2, 1, pack2)
    edges2 = [remote(8, y2send.at[0], y2recv.at[1], (g, below)), remote(9, y2send.at[1], y2recv.at[0], (g, above))]
    for copy in edges2:
        copy.start()
    ring_pass(old_ring)

    face_flux(refs, 1, False)
    over_planes(0, 4, 1, lambda i: plane_pair(refs, 2 * i + 1, range(1, YT - 1), False))
    for copy in edges2:
        copy.wait_recv()

    def unpack2(x):
        for odd in range(2):
            for j in range(NZT):
                for side, row, real in ((0, Y0 - 1, d > 0), (1, Y0 + BY, d < n_d - 1)):
                    t1[2 * x + odd + 1, j, pl.ds(row, 1), :] = jnp.where(
                        real, y2recv[side, x, pl.ds(odd * NZT + j, 1), :], 0.0
                    )

    over_planes(0, BX // 2, 1, unpack2)
    for i in range(4):
        for yt in (0, YT - 1):
            plane_pair(refs, 2 * i + 1, (yt,), False)
    over_planes(4, BX // 2 - 1, 1, lambda i: plane_pair(refs, 2 * i + 1, range(YT), False))
    for copy in faces2:
        copy.wait()
    for plane, outside in ((0, g == 0), (BX + 1, g == n_g - 1)):

        @pl.when(outside)
        def _():
            for j in range(NZT):
                for yt in range(YT):
                    t1[plane, j, pl.ds(Y0 + 8 * yt, 8), :] = jnp.zeros((8, 128), F32)

    for x in (0, BX - 1):
        outer_plane(refs, x, False)

    cut_list(h1, tl_ref, turned, put_into(new_out))
    ring_open(new_ring)
    stores = []
    for j in range(NZT):
        z = pl.ds(128 * j, 128)
        stores.append(pltpu.make_async_copy(h1.at[:, j], h_out.at[:, :, :, z], load_sem.at[j]))
        stores.append(pltpu.make_async_copy(h0.at[:, j], s_out.at[:, :, :, z], load_sem.at[NZT + j]))
    for copy in stores:
        copy.start()
    ring_close(old_ring)
    ring_pass(new_ring)
    ring_close(new_ring)
    for copy in stores:
        copy.wait()
    for copy in faces + edges + edges2:
        copy.wait_send()
    for copy in tables:
        copy.wait()


PZ = 10 * 32
PAD_ROWS = 18 * PZ
CUT = 80 * 16


def at_row(z, x, y):
    return (z + 1) * PZ + (x + 1) * 32 + y + 8


def permute(v, index, mask):
    return jnp.where(mask, jnp.take_along_axis(v, index, axis=1, mode="promise_in_bounds"), 0.0)


def ghosts(buf, index, mask):
    def planes(i, carry):
        made = []
        for u in range(4):
            z = 4 * i + u
            for yy in range(2):
                for face, src, dst in ((0, 7, -1), (1, 0, 8)):
                    v = permute(buf[pl.ds(at_row(z, src, 8 * yy), 8), :], index[face], mask[face])
                    made.append((pl.ds(at_row(z, dst, 8 * yy), 8), v))
            for face, src, dst in ((2, 15, -1), (3, 0, 16)):
                v = permute(buf[pl.ds(at_row(z, 0, src), 8, stride=32), :], index[face], mask[face])
                made.append((pl.ds(at_row(z, 0, dst), 8, stride=32), v))
        for rows, v in made:
            buf[rows, :] = v
        return carry

    lax.fori_loop(0, 4, planes, 0)
    made = []
    for x in range(8):
        for yy in range(2):
            for face, src, dst in ((4, 15, -1), (5, 0, 16)):
                v = permute(buf[pl.ds(at_row(src, x, 8 * yy), 8), :], index[face], mask[face])
                made.append((pl.ds(at_row(dst, x, 8 * yy), 8), v))
    for rows, v in made:
        buf[rows, :] = v


def solve_kernel(
    h_ref, s_ref, old_ref, new_ref, nbs_ref, nbv_ref, tl_ref,
    h_out, s_out, p_out,
    old_c, new_c, kb, pa, pb, src, dg, fx, fy, fz, back, tmp, unit, field, hs, ss, sem,
):
    g, d = lax.axis_index("grp"), lax.axis_index("dev")
    core = d % 2
    ins = [pltpu.make_async_copy(h_ref, hs, sem.at[0]), pltpu.make_async_copy(s_ref, ss, sem.at[1])]
    for copy in ins:
        copy.start()

    first = jnp.int32(0)
    for c in range(2):
        start = jnp.int32(0)
        for q in range(4):
            count = nbs_ref[c * 4 + q, 0, 6]

            def move(i, carry, c=c, q=q, start=start):
                to = pl.multiple_of((c * 32 + start + i) * 16, 16)
                at = pl.multiple_of(i * 16, 16)
                for half in range(2):
                    old_c[pl.ds(half * CUT + to, 16), :] = old_ref[c, q, half, pl.ds(at, 16), :]
                    new_c[pl.ds(half * CUT + to, 16), :] = new_ref[c, q, half, pl.ds(at, 16), :]
                return carry

            lax.fori_loop(0, count, move, 0)
            first = jnp.where((g == q) & (core == c), c * 32 + start, first)
            start = start + count

    def turned(ref, z):
        halves = [ref[pl.ds(half * CUT + z, 64, stride=16), :] for half in range(2)]
        return jnp.concatenate(halves, axis=0).T

    def spread(i, carry):
        for u in range(2):
            z = 2 * i + u
            old, new = turned(old_c, z), turned(new_c, z)
            rest = 1.0 - new
            perm = 0.5 * new * new * new / (rest * rest + 0.05)
            src[pl.ds(pl.multiple_of(z * 128, 128), 128), :] = (old - new) * RATE
            for x in range(8):
                kb[pl.ds(at_row(z, x, 0), 16), :] = perm[16 * x : 16 * x + 16, :]
        return carry

    lax.fori_loop(0, 8, spread, 0)

    order = [nbv_ref[c * 4 + (blk + 2) % 4] for c in range(2) for blk in range(4)]
    table = jnp.concatenate(order + order, axis=0).astype(F32).T.astype(jnp.int32)
    lane = lanes()
    lane_half, lane_q = lane // 64, lane % 64
    index, mask = [], []
    for face in range(6):
        n = jnp.broadcast_to(table[face : face + 1, :], (8, 128))
        real = n >= 0
        n = jnp.maximum(n, 0)
        owner = n // 8
        q = (owner % 2) * 32 + ((owner // 32 + 2) % 4) * 8 + n % 8
        if face == 0:
            q, real = jnp.where(lane_half == 1, lane_q, q + 64), (lane_half == 1) | real
        elif face == 1:
            q, real = jnp.where(lane_half == 0, lane_q + 64, q), (lane_half == 0) | real
        else:
            q = q + 64 * lane_half
        index.append(q)
        mask.append(real)

    outs = [pltpu.make_async_copy(hs, h_out, sem.at[0]), pltpu.make_async_copy(ss, s_out, sem.at[1])]
    for before, after in zip(ins, outs):
        before.wait()
        after.start()
    ghosts(kb, index, mask)

    def each(body):
        def planes(i, carry):
            for u in range(2):
                for x in range(8):
                    for yy in range(2):
                        body(2 * i + u, x, yy)
            return carry

        lax.fori_loop(0, 8, planes, 0)

    def k_at(z, x, y):
        return kb[pl.ds(at_row(z, x, y), 8), :]

    def flat(z, x, yy, xs=8, ys=16):
        return pl.ds((z * xs + x) * ys + 8 * yy, 8)

    def coefficients(z, x, yy):
        mid = k_at(z, x, 8 * yy)
        up = 0.5 * (mid + k_at(z, x + 1, 8 * yy))
        fx[flat(z, x + 1, yy, 9), :] = up
        down = 0.5 * (mid + k_at(z, x - 1, 8 * yy))
        if x == 0:
            fx[flat(z, 0, yy, 9), :] = down
        yup = 0.5 * (mid + k_at(z, x, 8 * yy + 1))
        ydown = 0.5 * (mid + k_at(z, x, 8 * yy - 1))
        if yy == 0:
            fy[pl.ds((z * 8 + x) * 24, 8), :] = ydown
        fy[pl.ds((z * 8 + x) * 24 + 8 * yy + 1, 8), :] = yup
        zup = 0.5 * (mid + k_at(z + 1, x, 8 * yy))
        zdown = 0.5 * (mid + k_at(z - 1, x, 8 * yy))
        fz[flat(z + 1, x, yy), :] = zup
        fz[flat(z, x, yy), :] = zdown
        inverse = 1.0 / (1.0 + (down + up + ydown + yup + zdown + zup))
        dg[flat(z, x, yy), :] = inverse
        pa[pl.ds(at_row(z, x, 8 * yy), 8), :] = src[flat(z, x, yy), :] * inverse

    each(coefficients)

    def sweep(a, b):
        ghosts(a, index, mask)

        def cell(z, x, yy):
            def p(dz, dx, dy):
                return a[pl.ds(at_row(z + dz, x + dx, 8 * yy + dy), 8), :]

            total = src[flat(z, x, yy), :]
            total += fx[flat(z, x, yy, 9), :] * p(0, -1, 0) + fx[flat(z, x + 1, yy, 9), :] * p(0, 1, 0)
            low = (z * 8 + x) * 24 + 8 * yy
            total += fy[pl.ds(low, 8), :] * p(0, 0, -1) + fy[pl.ds(low + 1, 8), :] * p(0, 0, 1)
            total += fz[flat(z, x, yy), :] * p(-1, 0, 0) + fz[flat(z + 1, x, yy), :] * p(1, 0, 0)
            b[pl.ds(at_row(z, x, 8 * yy), 8), :] = total * dg[flat(z, x, yy), :]

        each(cell)

    sweep(pa, pb)
    sweep(pb, pa)
    sweep(pa, pb)

    def turn_back(i, carry):
        for u in range(4):
            z = 4 * i + u
            rows = [pb[pl.ds(at_row(z, x, 0), 16), :] for x in range(8)]
            back[pl.ds(pl.multiple_of(z * 144, 8), 128), :] = jnp.concatenate(rows, axis=0).T
        return carry

    lax.fori_loop(0, 4, turn_back, 0)

    def blank(x, carry):
        for j in range(NZT):
            field[x, j] = jnp.zeros((BY, 128), F32)
        return carry

    lax.fori_loop(0, BX, blank, 0)

    for group in range(2):
        for half in range(2):
            for z in range(16):
                v = back[pl.ds(z * 144 + half * 64 + first + group * 8, 8), :]
                tmp[pl.ds(z, 8, stride=16), :] = v
            unit[pl.ds((group * 2 + half) * 128, 128), :] = tmp[...].T

    block = lanes() // 16
    listed = nbs_ref[core * 4 + g, 0, 6]

    def place(i, carry):
        t = tl_ref[0, i]
        x0 = (t // 128) * 16
        y0 = pl.multiple_of(((t // 32) % 4) * 16, 16)
        tz = t % 32
        zt, slot = tz // 8, tz % 8
        shift = (slot * 16 - (i % 8) * 16 + 128) % 128
        made = []
        for half in range(2):
            for x in range(8):
                for yy in range(2):
                    row = pl.multiple_of((i // 8 * 2 + half) * 128 + x * 16 + 8 * yy, 8)
                    v = pltpu.roll(unit[pl.ds(row, 8), :], shift, 1)
                    spot = (x0 + half * 8 + x, zt, pl.ds(y0 + 8 * yy, 8))
                    made.append((spot, jnp.where(block == slot, v, field[spot])))
        for spot, v in made:
            field[spot] = v
        return carry

    lax.fori_loop(0, listed, place, 0)
    stores = [pltpu.make_async_copy(field.at[:, j], p_out.at[:, :, pl.ds(128 * j, 128)], sem.at[2 + j]) for j in range(NZT)]
    for copy in stores:
        copy.start()
    for copy in stores + outs:
        copy.wait()


VM = pl.BlockSpec(memory_space=pltpu.VMEM)
SM = pl.BlockSpec(memory_space=pltpu.SMEM)
ANY = pl.BlockSpec(memory_space=pl.ANY)


def solve_call(h_new, shrink, old_l, new_l, table, tile_list):
    brick = jax.ShapeDtypeStruct((BX, BY, BZ), F32)
    cells = (BX, NZT, BY, 128)
    return pl.pallas_call(
        solve_kernel,
        out_shape=[brick, brick, brick],
        in_specs=[ANY, ANY, VM, VM, SM, VM, SM],
        out_specs=[ANY, ANY, ANY],
        scratch_shapes=[
            pltpu.VMEM((2 * CUT, 128), F32),
            pltpu.VMEM((2 * CUT, 128), F32),
            pltpu.VMEM((PAD_ROWS, 128), F32),
            pltpu.VMEM((PAD_ROWS, 128), F32),
            pltpu.VMEM((PAD_ROWS, 128), F32),
            pltpu.VMEM((2048, 128), F32),
            pltpu.VMEM((2048, 128), F32),
            pltpu.VMEM((16 * 9 * 16, 128), F32),
            pltpu.VMEM((16 * 8 * 24, 128), F32),
            pltpu.VMEM((17 * 8 * 16, 128), F32),
            pltpu.VMEM((16 * 144, 128), F32),
            pltpu.VMEM((128, 128), F32),
            pltpu.VMEM((512, 128), F32),
            pltpu.VMEM(cells, F32),
            pltpu.VMEM((BX, BY, BZ), F32),
            pltpu.VMEM((BX, BY, BZ), F32),
            pltpu.SemaphoreType.DMA((2 + NZT,)),
        ],
        compiler_params=pltpu.CompilerParams(vmem_limit_bytes=50 * 2**20),
        cost_estimate=pl.CostEstimate(flops=20 * 2**20, bytes_accessed=40 * 2**20, transcendentals=0),
        name="solve_tiles",
    )(h_new, shrink, old_l, new_l, table, table, tile_list)


def heat_call(enthalpy, conduct, tile_count, tile_list, neighbours):
    brick = jax.ShapeDtypeStruct((BX, YT, 8, BZ), F32)
    lists = jax.ShapeDtypeStruct((2, 4, 2, 256, 128), F32)
    cells = (BX, NZT, YT, 8, 128)
    padded = (BX + 2, NZT, YP, 128)
    return pl.pallas_call(
        heat_kernel,
        out_shape=[brick, brick, lists, lists, jax.ShapeDtypeStruct((8, 8, 128), jnp.int32)],
        in_specs=[ANY, ANY, SM, SM, VM],
        out_specs=[ANY, ANY, VM, VM, VM],
        scratch_shapes=[
            pltpu.VMEM(cells, F32),
            pltpu.VMEM(cells, F32),
            pltpu.VMEM(padded, F32),
            pltpu.VMEM(padded, F32),
            pltpu.VMEM(padded, F32),
            pltpu.VMEM(cells, F32),
            pltpu.VMEM((NZT, YT, 8, 128), F32),
            pltpu.VMEM((2, YT, 8, BZ), F32),
            pltpu.VMEM((2, BY, BZ), F32),
            pltpu.VMEM((2, BX, 2 * NZT, 128), F32),
            pltpu.VMEM((2, BX, 2 * NZT, 128), F32),
            pltpu.VMEM((2, BX // 2, 2 * NZT, 128), F32),
            pltpu.VMEM((2, BX // 2, 2 * NZT, 128), F32),
            pltpu.VMEM((2, 16, 8, 128), F32),
            pltpu.SemaphoreType.DMA((2 * NZT,)),
            pltpu.SemaphoreType.DMA((60,)),
            pltpu.SemaphoreType.DMA((60,)),
        ],
        compiler_params=pltpu.CompilerParams(collective_id=0, has_side_effects=True, vmem_limit_bytes=50 * 2**20),
        cost_estimate=pl.CostEstimate(flops=80 * BX * BY * BZ, bytes_accessed=20 * 2**20, transcendentals=0),
        name="heat_steps",
    )(enthalpy.reshape(BX, YT, 8, BZ), conduct, tile_count, tile_list, neighbours)


def local(enthalpy, conduct, tile_count, tile_list, neighbours):
    h_new, shrink, old_l, new_l, table = heat_call(enthalpy, conduct, tile_count, tile_list, neighbours)
    return solve_call(h_new.reshape(BX, BY, BZ), shrink.reshape(BX, BY, BZ), old_l, new_l, table, tile_list)


def solution(mesh):
    placed = (
        P("grp", "dev", None),
        P("grp", "dev", None),
        P(("grp", "dev")),
        P(("grp", "dev"), None),
        P(("grp", "dev"), None),
    )
    return jax.shard_map(
        local,
        mesh=mesh,
        in_specs=placed,
        out_specs=(P("grp", "dev", None), P("grp", "dev", None), P("grp", "dev", None)),
        check_vma=False,
    )
```

```python
import functools

import jax
import jax.numpy as jnp
from jax import lax
from jax.experimental import pallas as pl
from jax.experimental.pallas import tpu as pltpu
from jax.sharding import PartitionSpec as P

MESH = pl.DeviceIdType.MESH
F32 = jnp.float32
BX, BY, BZ = 32, 64, 512
NZT = BZ // 128
CHUNKS = 4
CHUNK = BX // CHUNKS
YT = BY // 8
HEAT = 0.15
FLUX = 0.5 * HEAT
RATE = 1.0 / (2 * HEAT)
LISTED = 16
MIDDLE = 17
Y0 = 8
YP = BY + 2 * Y0


def clip01(v):
    return jnp.minimum(jnp.maximum(v, 0.0), 1.0)


def temper(v):
    return v - clip01(v)


def lanes():
    return lax.broadcasted_iota(jnp.int32, (8, 128), 1)


def up_z(row, end):
    first = lanes() == 127
    rolled = [pltpu.roll(v, 127, 1) for v in row]
    return [jnp.where(first, rolled[j + 1] if j + 1 < len(row) else end, rolled[j]) for j in range(len(row))]


def down_z(row, before):
    last = lanes() == 0
    rolled = [pltpu.roll(v, 1, 1) for v in row]
    return [jnp.where(last, rolled[j - 1] if j else before, rolled[j]) for j in range(len(row))]


def flux_row(t_ref, k_ref, kz_ref, x, yt):
    xp = x + 1
    lo = Y0 + 8 * yt
    mid = pl.ds(lo, 8)
    zts = range(NZT)
    t = [t_ref[xp, j, mid, :] for j in zts]
    k = [k_ref[xp, j, mid, :] for j in zts]
    tz = up_z(t, 0.0)
    kz = [kz_ref[x, j, yt] for j in zts]
    fz = [kz[j] * (tz[j] - t[j]) for j in zts]
    fzm = down_z(fz, k[0] * t[0])
    out = []
    for j in zts:
        acc = fz[j] - fzm[j]
        for dx, dy in ((1, 0), (-1, 0), (0, 1), (0, -1)):
            rows = pl.ds(lo + dy, 8)
            acc = acc + (k[j] + k_ref[xp + dx, j, rows, :]) * (t_ref[xp + dx, j, rows, :] - t[j])
        out.append(acc)
    return out


def finish(refs, x, yt, acc, first):
    h0, h1, kp, t0, t1, kz, fx = refs
    for j in range(NZT):
        if first:
            new = h0[x, j, yt] + FLUX * acc[j]
            t1[x + 1, j, pl.ds(Y0 + 8 * yt, 8), :] = temper(new)
        else:
            new = h1[x, j, yt] + FLUX * acc[j]
            h0[x, j, yt] = (clip01(h0[x, j, yt]) - clip01(new)) * RATE
        h1[x, j, yt] = new


def outer_plane(refs, x, first):
    h0, h1, kp, t0, t1, kz, fx = refs
    for yt in range(YT):
        finish(refs, x, yt, flux_row(t0 if first else t1, kp, kz, x, yt), first)


def face_flux(refs, x, first):
    h0, h1, kp, t0, t1, kz, fx = refs
    t_ref = t0 if first else t1
    for yt in range(YT):
        rows = pl.ds(Y0 + 8 * yt, 8)
        for j in range(NZT):
            fx[j, yt] = (kp[x, j, rows, :] + kp[x + 1, j, rows, :]) * (t_ref[x + 1, j, rows, :] - t_ref[x, j, rows, :])


def plane_pair(refs, x, yts, first):
    h0, h1, kp, t0, t1, kz, fx = refs
    t_ref = t0 if first else t1
    zts = range(NZT)
    for yt in yts:
        lo = Y0 + 8 * yt
        rows = pl.ds(lo, 8)
        t = [[t_ref[x + 1 + p, j, rows, :] for j in zts] for p in range(3)]
        k = [[kp[x + 1 + p, j, rows, :] for j in zts] for p in range(3)]
        face = [[fx[j, yt] for j in zts]]
        for p in range(2):
            face.append([(k[p][j] + k[p + 1][j]) * (t[p + 1][j] - t[p][j]) for j in zts])
        for j in zts:
            fx[j, yt] = face[2][j]
        for p in range(2):
            xp = x + p
            acc = [face[p + 1][j] - face[p][j] for j in zts]
            for dy in (1, -1):
                side = pl.ds(lo + dy, 8)
                acc = [acc[j] + (k[p][j] + kp[xp + 1, j, side, :]) * (t_ref[xp + 1, j, side, :] - t[p][j]) for j in zts]
            tz = up_z(t[p], 0.0)
            kzs = [kz[xp, j, yt] for j in zts]
            fz = [kzs[j] * (tz[j] - t[p][j]) for j in zts]
            fzm = down_z(fz, k[p][0] * t[p][0])
            finish(refs, xp, yt, [acc[j] + (fz[j] - fzm[j]) for j in zts], first)


def over_planes(low, high, step, body):
    def one(i, carry):
        body(i)
        return carry

    lax.fori_loop(low, high, one, 0)


def cut_list(src, tl_ref, turned, half, put):
    def part(n, carry):
        for u in range(2):
            i = 2 * n + u
            t = tl_ref[0, i]
            x0, y0, zt, at = (t >> 7) * 16, ((t >> 5) & 3) * 2, (t & 31) >> 3, (t & 7) * 2
            block = [src[x0 + half * 8 + x, zt, y0 + yy] for x in range(8) for yy in range(2)]
            turned[u] = clip01(jnp.concatenate(block, axis=0)).T.reshape(16, 8, 128)
            for q in range(2):
                put(half, i * 16 + q * 8, turned[u, at + q])
        return carry

    lax.fori_loop(0, LISTED // 2, part, 0)


def heat_kernel(
    h_ref, k_ref, tc_ref, tl_hbm, nb_hbm,
    h_out, s_out, old_out, new_out, nb_out,
    h0, h1, kp, t0, t1, kz, fx, hx, kx, ysend, yrecv, y2send, y2recv, turned, tl_ref, nb_ref, load_sem, send_sem, recv_sem,
):
    g, d = lax.axis_index("grp"), lax.axis_index("dev")
    n_g, n_d = lax.axis_size("grp"), lax.axis_size("dev")
    core = d % 2
    mate = d + 1 - 2 * core
    right, left = (g + 1) % n_g, (g + n_g - 1) % n_g
    above, below = (d + 1) % n_d, (d + n_d - 1) % n_d
    aside = (d + n_d + 2 * core - 1) % n_d

    small = [
        pltpu.make_async_copy(tl_hbm, tl_ref, load_sem.at[CHUNKS, 0]),
        pltpu.make_async_copy(nb_hbm, nb_ref, load_sem.at[CHUNKS, 1]),
    ]
    for copy in small:
        copy.start()
    loads = []
    for c in range(CHUNKS):
        planes = pl.ds(c * CHUNK, CHUNK)
        part = []
        for j in range(NZT):
            z = pl.ds(128 * j, 128)
            part.append(pltpu.make_async_copy(h_ref.at[planes, :, :, z], h0.at[planes, j], load_sem.at[c, j]))
            part.append(
                pltpu.make_async_copy(
                    k_ref.at[planes, :, z], kp.at[pl.ds(1 + c * CHUNK, CHUNK), j, pl.ds(Y0, BY), :], load_sem.at[c, NZT + j]
                )
            )
        loads.append(part)
    for part in loads:
        for copy in part:
            copy.start()

    barrier = pltpu.get_barrier_semaphore()
    pair = [((g + dg) % n_g, mate if dc else d) for dg in range(4) for dc in range(2) if dg or dc]
    for peer in pair + [(g, aside)]:
        pl.semaphore_signal(barrier, inc=1, device_id=peer, device_id_type=MESH)
    pl.semaphore_wait(barrier, 8)

    def remote(n, src, dst, peer):
        return pltpu.make_async_remote_copy(
            src_ref=src, dst_ref=dst, send_sem=send_sem.at[n], recv_sem=recv_sem.at[n], device_id=peer, device_id_type=MESH
        )

    faces = [
        remote(0, h_ref.at[0], hx.at[1], (left, d)),
        remote(1, h_ref.at[BX - 1], hx.at[0], (right, d)),
        remote(2, k_ref.at[0], kx.at[1], (left, d)),
        remote(3, k_ref.at[BX - 1], kx.at[0], (right, d)),
    ]
    for copy in faces:
        copy.start()

    for copy in small:
        copy.wait()
    column = lax.broadcasted_iota(jnp.int32, (8, 128), 1)
    mine = nb_out.at[core * 4 + g]
    nb_out[core * 4 + g] = jnp.where(column == 6, tc_ref[0], jnp.zeros((8, 128), jnp.int32))
    nb_out[core * 4 + g, :, 0:6] = nb_ref[...]
    tables = [remote(10 + n, mine, mine, peer) for n, peer in enumerate(pair)]
    for copy in tables:
        copy.start()

    def pack(x):
        for j in range(NZT):
            for side, row in ((0, 0), (1, BY - 1)):
                ysend[side, x, pl.ds(j, 1), :] = h0[x, j, row // 8, pl.ds(row % 8, 1), :]
                ysend[side, x, pl.ds(NZT + j, 1), :] = kp[x + 1, j, pl.ds(Y0 + row, 1), :]

    def warm(i):
        for u in range(4):
            x = 4 * i + u
            for yt in range(YT):
                rows = pl.ds(Y0 + 8 * yt, 8)
                k = [kp[x + 1, j, rows, :] for j in range(NZT)]
                above_k = up_z(k, 0.0)
                for j in range(NZT):
                    kz[x, j, yt] = k[j] + above_k[j]
                    t0[x + 1, j, rows, :] = temper(h0[x, j, yt])
            pack(x)

    for c, part in enumerate(loads):
        for copy in part:
            copy.wait()
        over_planes(c * CHUNK // 4, (c + 1) * CHUNK // 4, 1, warm)

    edges = [remote(4, ysend.at[0], yrecv.at[1], (g, below)), remote(5, ysend.at[1], yrecv.at[0], (g, above))]
    for copy in edges:
        copy.start()

    def ring(base, buf):
        own = buf.at[core, g]
        from_left, from_right, far = buf.at[core, left], buf.at[core, right], buf.at[core, (g + 2) % n_g]
        return dict(
            first=[
                remote(base + 0, own.at[0], own.at[0], (right, d)),
                remote(base + 1, own.at[0], own.at[0], (left, d)),
                remote(base + 2, own.at[1], own.at[1], (right, d)),
                remote(base + 3, own.at[1], own.at[1], (left, d)),
            ],
            onward=[
                remote(base + 4, from_left.at[0], from_left.at[0], (right, d)),
                remote(base + 5, from_right.at[1], from_right.at[1], (left, d)),
            ],
            mate=[
                remote(base + 6, own.at[0], own.at[0], (g, mate)),
                remote(base + 7, own.at[1], own.at[1], (g, mate)),
                remote(base + 8, from_left.at[0], from_left.at[0], (g, mate)),
                remote(base + 9, from_right.at[0], from_right.at[0], (g, mate)),
                remote(base + 10, from_left.at[1], from_left.at[1], (g, mate)),
                remote(base + 11, from_right.at[1], from_right.at[1], (g, mate)),
                remote(base + 12, far.at[0], far.at[0], (g, mate)),
                remote(base + 13, far.at[1], far.at[1], (g, mate)),
            ],
        )

    def ring_open(r, half):
        for copy in r["first"][2 * half : 2 * half + 2]:
            copy.start()
        r["mate"][half].start()

    def ring_pass(r):
        first, onward, pass_on = r["first"], r["onward"], r["mate"]
        first[0].wait_recv()
        onward[0].start()
        pass_on[2].start()
        first[1].wait_recv()
        pass_on[3].start()
        first[3].wait_recv()
        onward[1].start()
        pass_on[5].start()
        first[2].wait_recv()
        pass_on[4].start()

    def ring_close(r):
        for n in range(2):
            r["onward"][n].wait_recv()
            r["mate"][6 + n].start()
        for copy in r["mate"]:
            copy.wait_recv()
        for copy in r["first"] + r["onward"] + r["mate"]:
            copy.wait_send()

    def put_into(buf):
        def put(half, row, value):
            buf[core, g, half, pl.ds(pl.multiple_of(row, 8), 8), :] = value

        return put

    old_ring, new_ring = ring(20, old_out), ring(40, new_out)
    for half in range(2):
        cut_list(h0, tl_ref, turned, half, put_into(old_out))
    for half in range(2):
        ring_open(old_ring, half)
    refs = (h0, h1, kp, t0, t1, kz, fx)

    def pairs(low, high, yts, first):
        over_planes(low // 2, high // 2, 1, lambda i: plane_pair(refs, 2 * i + low % 2, yts, first))

    whole, inner = range(YT), range(1, YT - 1)

    for copy in edges:
        copy.wait_recv()

    def unpack(x):
        for j in range(NZT):
            for side, row, real in ((0, Y0 - 1, d > 0), (1, Y0 + BY, d < n_d - 1)):
                t0[x + 1, j, pl.ds(row, 1), :] = jnp.where(real, temper(yrecv[side, x, pl.ds(j, 1), :]), 0.0)
                kp[x + 1, j, pl.ds(row, 1), :] = jnp.where(real, yrecv[side, x, pl.ds(NZT + j, 1), :], 0.0)

    over_planes(0, BX, 1, unpack)

    face_flux(refs, 1, True)
    pairs(1, MIDDLE, whole, True)
    for copy in faces:
        copy.wait_recv()
    for side, plane, real in ((0, 0, g > 0), (1, BX + 1, g < n_g - 1)):
        for j in range(NZT):
            z = pl.ds(128 * j, 128)
            for yt in range(YT):
                rows = pl.ds(8 * yt, 8)
                t0[plane, j, pl.ds(Y0 + 8 * yt, 8), :] = jnp.where(real, temper(hx[side, yt, :, z]), 0.0)
                kp[plane, j, pl.ds(Y0 + 8 * yt, 8), :] = jnp.where(real, kx[side, rows, z], 0.0)
    for x in (0, BX - 1):
        outer_plane(refs, x, True)

    inside = pl.ds(Y0, BY)
    faces2 = [
        remote(6, t1.at[1, :, inside, :], t1.at[BX + 1, :, inside, :], (left, d)),
        remote(7, t1.at[BX, :, inside, :], t1.at[0, :, inside, :], (right, d)),
    ]
    for copy in faces2:
        copy.start()
    pairs(MIDDLE, BX - 1, whole, True)

    def pack2(x):
        for odd in range(2):
            for j in range(NZT):
                for side, row in ((0, Y0), (1, Y0 + BY - 1)):
                    y2send[side, x, pl.ds(odd * NZT + j, 1), :] = t1[2 * x + odd + 1, j, pl.ds(row, 1), :]

    over_planes(0, BX // 2, 1, pack2)
    edges2 = [remote(8, y2send.at[0], y2recv.at[1], (g, below)), remote(9, y2send.at[1], y2recv.at[0], (g, above))]
    for copy in edges2:
        copy.start()
    ring_pass(old_ring)

    face_flux(refs, 16, False)
    pairs(16, 24, inner, False)
    for copy in edges2:
        copy.wait_recv()

    def unpack2(x):
        for odd in range(2):
            for j in range(NZT):
                for side, row, real in ((0, Y0 - 1, d > 0), (1, Y0 + BY, d < n_d - 1)):
                    t1[2 * x + odd + 1, j, pl.ds(row, 1), :] = jnp.where(
                        real, y2recv[side, x, pl.ds(odd * NZT + j, 1), :], 0.0
                    )

    over_planes(0, BX // 2, 1, unpack2)
    for x in range(16, 24, 2):
        for yt in (0, YT - 1):
            plane_pair(refs, x, (yt,), False)

    for copy in faces2:
        copy.wait()
    for plane, outside in ((0, g == 0), (BX + 1, g == n_g - 1)):

        @pl.when(outside)
        def _():
            for j in range(NZT):
                for yt in range(YT):
                    t1[plane, j, pl.ds(Y0 + 8 * yt, 8), :] = jnp.zeros((8, 128), F32)

    face_flux(refs, 0, False)
    pairs(0, 8, whole, False)
    cut_list(h1, tl_ref, turned, 0, put_into(new_out))
    ring_open(new_ring, 0)
    pairs(8, 16, whole, False)
    face_flux(refs, 24, False)
    pairs(24, BX, whole, False)
    cut_list(h1, tl_ref, turned, 1, put_into(new_out))
    ring_open(new_ring, 1)

    stores = []
    for j in range(NZT):
        z = pl.ds(128 * j, 128)
        stores.append(pltpu.make_async_copy(h1.at[:, j], h_out.at[:, :, :, z], load_sem.at[0, j]))
        stores.append(pltpu.make_async_copy(h0.at[:, j], s_out.at[:, :, :, z], load_sem.at[0, NZT + j]))
    for copy in stores:
        copy.start()
    ring_close(old_ring)
    ring_pass(new_ring)
    ring_close(new_ring)
    for copy in stores:
        copy.wait()
    for copy in faces + edges + edges2:
        copy.wait_send()
    for copy in tables:
        copy.wait()


PZ = 10 * 32
PAD_ROWS = 18 * PZ
CUT = 80 * 16


def at_row(z, x, y):
    return (z + 1) * PZ + (x + 1) * 32 + y + 8


def permute(v, index, mask):
    return jnp.where(mask, jnp.take_along_axis(v, index, axis=1, mode="promise_in_bounds"), 0.0)


def ghosts(buf, index, mask):
    def planes(i, carry):
        made = []
        for u in range(4):
            z = 4 * i + u
            for yy in range(2):
                for face, src, dst in ((0, 7, -1), (1, 0, 8)):
                    v = permute(buf[pl.ds(at_row(z, src, 8 * yy), 8), :], index[face], mask[face])
                    made.append((pl.ds(at_row(z, dst, 8 * yy), 8), v))
            for face, src, dst in ((2, 15, -1), (3, 0, 16)):
                v = permute(buf[pl.ds(at_row(z, 0, src), 8, stride=32), :], index[face], mask[face])
                made.append((pl.ds(at_row(z, 0, dst), 8, stride=32), v))
        for rows, v in made:
            buf[rows, :] = v
        return carry

    lax.fori_loop(0, 4, planes, 0)
    made = []
    for x in range(8):
        for yy in range(2):
            for face, src, dst in ((4, 15, -1), (5, 0, 16)):
                v = permute(buf[pl.ds(at_row(src, x, 8 * yy), 8), :], index[face], mask[face])
                made.append((pl.ds(at_row(dst, x, 8 * yy), 8), v))
    for rows, v in made:
        buf[rows, :] = v


def solve_kernel(
    h_ref, s_ref, old_ref, new_ref, nbs_ref, nbv_ref, tl_hbm,
    h_out, s_out, p_out,
    old_c, new_c, kb, pa, pb, src, dg, fx, fy, fz, back, tmp, unit, field, hs, ss, tl_ref, sem,
):
    g, d = lax.axis_index("grp"), lax.axis_index("dev")
    core = d % 2
    listing = pltpu.make_async_copy(tl_hbm, tl_ref, sem.at[2 + NZT])
    listing.start()
    ins = [pltpu.make_async_copy(h_ref, hs, sem.at[0]), pltpu.make_async_copy(s_ref, ss, sem.at[1])]
    for copy in ins:
        copy.start()

    first = jnp.int32(0)
    for c in range(2):
        start = jnp.int32(0)
        for q in range(4):
            count = nbs_ref[c * 4 + q, 0, 6]

            def move(i, carry, c=c, q=q, start=start):
                to = pl.multiple_of((c * 32 + start + i) * 16, 16)
                at = pl.multiple_of(i * 16, 16)
                for half in range(2):
                    old_c[pl.ds(half * CUT + to, 16), :] = old_ref[c, q, half, pl.ds(at, 16), :]
                    new_c[pl.ds(half * CUT + to, 16), :] = new_ref[c, q, half, pl.ds(at, 16), :]
                return carry

            lax.fori_loop(0, count, move, 0)
            first = jnp.where((g == q) & (core == c), c * 32 + start, first)
            start = start + count

    def turned(ref, z):
        halves = [ref[pl.ds(half * CUT + z, 64, stride=16), :] for half in range(2)]
        return jnp.concatenate(halves, axis=0).T

    def spread(i, carry):
        for u in range(2):
            z = 2 * i + u
            old, new = turned(old_c, z), turned(new_c, z)
            rest = 1.0 - new
            perm = 0.5 * new * new * new / (rest * rest + 0.05)
            src[pl.ds(pl.multiple_of(z * 128, 128), 128), :] = (old - new) * RATE
            for x in range(8):
                kb[pl.ds(at_row(z, x, 0), 16), :] = perm[16 * x : 16 * x + 16, :]
        return carry

    lax.fori_loop(0, 8, spread, 0)

    order = [nbv_ref[c * 4 + (blk + 2) % 4] for c in range(2) for blk in range(4)]
    table = jnp.concatenate(order + order, axis=0).astype(F32).T.astype(jnp.int32)
    lane = lanes()
    lane_half, lane_q = lane // 64, lane % 64
    index, mask = [], []
    for face in range(6):
        n = jnp.broadcast_to(table[face : face + 1, :], (8, 128))
        real = n >= 0
        n = jnp.maximum(n, 0)
        owner = n // 8
        q = (owner % 2) * 32 + ((owner // 32 + 2) % 4) * 8 + n % 8
        if face == 0:
            q, real = jnp.where(lane_half == 1, lane_q, q + 64), (lane_half == 1) | real
        elif face == 1:
            q, real = jnp.where(lane_half == 0, lane_q + 64, q), (lane_half == 0) | real
        else:
            q = q + 64 * lane_half
        index.append(q)
        mask.append(real)

    outs = [pltpu.make_async_copy(hs, h_out, sem.at[0]), pltpu.make_async_copy(ss, s_out, sem.at[1])]
    for before, after in zip(ins, outs):
        before.wait()
        after.start()
    ghosts(kb, index, mask)

    def each(body):
        def planes(i, carry):
            for u in range(2):
                for x in range(8):
                    for yy in range(2):
                        body(2 * i + u, x, yy)
            return carry

        lax.fori_loop(0, 8, planes, 0)

    def k_at(z, x, y):
        return kb[pl.ds(at_row(z, x, y), 8), :]

    def flat(z, x, yy, xs=8, ys=16):
        return pl.ds((z * xs + x) * ys + 8 * yy, 8)

    def coefficients(z, x, yy):
        mid = k_at(z, x, 8 * yy)
        up = 0.5 * (mid + k_at(z, x + 1, 8 * yy))
        fx[flat(z, x + 1, yy, 9), :] = up
        down = 0.5 * (mid + k_at(z, x - 1, 8 * yy))
        if x == 0:
            fx[flat(z, 0, yy, 9), :] = down
        yup = 0.5 * (mid + k_at(z, x, 8 * yy + 1))
        ydown = 0.5 * (mid + k_at(z, x, 8 * yy - 1))
        if yy == 0:
            fy[pl.ds((z * 8 + x) * 24, 8), :] = ydown
        fy[pl.ds((z * 8 + x) * 24 + 8 * yy + 1, 8), :] = yup
        zup = 0.5 * (mid + k_at(z + 1, x, 8 * yy))
        zdown = 0.5 * (mid + k_at(z - 1, x, 8 * yy))
        fz[flat(z + 1, x, yy), :] = zup
        fz[flat(z, x, yy), :] = zdown
        inverse = 1.0 / (1.0 + (down + up + ydown + yup + zdown + zup))
        dg[flat(z, x, yy), :] = inverse
        pa[pl.ds(at_row(z, x, 8 * yy), 8), :] = src[flat(z, x, yy), :] * inverse

    each(coefficients)

    def sweep(a, b):
        ghosts(a, index, mask)

        def cell(z, x, yy):
            def p(dz, dx, dy):
                return a[pl.ds(at_row(z + dz, x + dx, 8 * yy + dy), 8), :]

            total = src[flat(z, x, yy), :]
            total += fx[flat(z, x, yy, 9), :] * p(0, -1, 0) + fx[flat(z, x + 1, yy, 9), :] * p(0, 1, 0)
            low = (z * 8 + x) * 24 + 8 * yy
            total += fy[pl.ds(low, 8), :] * p(0, 0, -1) + fy[pl.ds(low + 1, 8), :] * p(0, 0, 1)
            total += fz[flat(z, x, yy), :] * p(-1, 0, 0) + fz[flat(z + 1, x, yy), :] * p(1, 0, 0)
            b[pl.ds(at_row(z, x, 8 * yy), 8), :] = total * dg[flat(z, x, yy), :]

        each(cell)

    sweep(pa, pb)
    sweep(pb, pa)
    sweep(pa, pb)

    def turn_back(i, carry):
        for u in range(4):
            z = 4 * i + u
            rows = [pb[pl.ds(at_row(z, x, 0), 16), :] for x in range(8)]
            back[pl.ds(pl.multiple_of(z * 144, 8), 128), :] = jnp.concatenate(rows, axis=0).T
        return carry

    lax.fori_loop(0, 4, turn_back, 0)

    def blank(x, carry):
        for j in range(NZT):
            field[x, j] = jnp.zeros((BY, 128), F32)
        return carry

    lax.fori_loop(0, BX, blank, 0)

    for group in range(2):
        for half in range(2):
            for z in range(16):
                v = back[pl.ds(z * 144 + half * 64 + first + group * 8, 8), :]
                tmp[pl.ds(z, 8, stride=16), :] = v
            unit[pl.ds((group * 2 + half) * 128, 128), :] = tmp[...].T

    listing.wait()
    block = lanes() // 16
    listed = nbs_ref[core * 4 + g, 0, 6]

    def place(i, carry):
        t = tl_ref[0, i]
        x0 = (t // 128) * 16
        y0 = pl.multiple_of(((t // 32) % 4) * 16, 16)
        tz = t % 32
        zt, slot = tz // 8, tz % 8
        shift = (slot * 16 - (i % 8) * 16 + 128) % 128
        made = []
        for half in range(2):
            for x in range(8):
                for yy in range(2):
                    row = pl.multiple_of((i // 8 * 2 + half) * 128 + x * 16 + 8 * yy, 8)
                    v = pltpu.roll(unit[pl.ds(row, 8), :], shift, 1)
                    spot = (x0 + half * 8 + x, zt, pl.ds(y0 + 8 * yy, 8))
                    made.append((spot, jnp.where(block == slot, v, field[spot])))
        for spot, v in made:
            field[spot] = v
        return carry

    lax.fori_loop(0, listed, place, 0)
    stores = [pltpu.make_async_copy(field.at[:, j], p_out.at[:, :, pl.ds(128 * j, 128)], sem.at[2 + j]) for j in range(NZT)]
    for copy in stores:
        copy.start()
    for copy in stores + outs:
        copy.wait()


VM = pl.BlockSpec(memory_space=pltpu.VMEM)
SM = pl.BlockSpec(memory_space=pltpu.SMEM)
ANY = pl.BlockSpec(memory_space=pl.ANY)
HB = pl.BlockSpec(memory_space=pltpu.HBM)


def solve_call(h_new, shrink, old_l, new_l, table, tile_list):
    brick = jax.ShapeDtypeStruct((BX, BY, BZ), F32)
    cells = (BX, NZT, BY, 128)
    return pl.pallas_call(
        solve_kernel,
        out_shape=[brick, brick, brick],
        in_specs=[ANY, ANY, VM, VM, SM, VM, HB],
        out_specs=[ANY, ANY, ANY],
        scratch_shapes=[
            pltpu.VMEM((2 * CUT, 128), F32),
            pltpu.VMEM((2 * CUT, 128), F32),
            pltpu.VMEM((PAD_ROWS, 128), F32),
            pltpu.VMEM((PAD_ROWS, 128), F32),
            pltpu.VMEM((PAD_ROWS, 128), F32),
            pltpu.VMEM((2048, 128), F32),
            pltpu.VMEM((2048, 128), F32),
            pltpu.VMEM((16 * 9 * 16, 128), F32),
            pltpu.VMEM((16 * 8 * 24, 128), F32),
            pltpu.VMEM((17 * 8 * 16, 128), F32),
            pltpu.VMEM((16 * 144, 128), F32),
            pltpu.VMEM((128, 128), F32),
            pltpu.VMEM((512, 128), F32),
            pltpu.VMEM(cells, F32),
            pltpu.VMEM((BX, BY, BZ), F32),
            pltpu.VMEM((BX, BY, BZ), F32),
            pltpu.SMEM((1, LISTED), jnp.int32),
            pltpu.SemaphoreType.DMA((3 + NZT,)),
        ],
        compiler_params=pltpu.CompilerParams(vmem_limit_bytes=36 * 2**20),
        cost_estimate=pl.CostEstimate(flops=20 * 2**20, bytes_accessed=40 * 2**20, transcendentals=0),
        name="solve_tiles",
    )(h_new, shrink, old_l, new_l, table, table, tile_list)


def heat_call(enthalpy, conduct, tile_count, tile_list, neighbours):
    brick = jax.ShapeDtypeStruct((BX, YT, 8, BZ), F32)
    lists = jax.ShapeDtypeStruct((2, 4, 2, 256, 128), F32)
    cells = (BX, NZT, YT, 8, 128)
    padded = (BX + 2, NZT, YP, 128)
    return pl.pallas_call(
        heat_kernel,
        out_shape=[brick, brick, lists, lists, jax.ShapeDtypeStruct((8, 8, 128), jnp.int32)],
        in_specs=[ANY, ANY, SM, HB, HB],
        out_specs=[ANY, ANY, VM, VM, VM],
        scratch_shapes=[
            pltpu.VMEM(cells, F32),
            pltpu.VMEM(cells, F32),
            pltpu.VMEM(padded, F32),
            pltpu.VMEM(padded, F32),
            pltpu.VMEM(padded, F32),
            pltpu.VMEM(cells, F32),
            pltpu.VMEM((NZT, YT, 8, 128), F32),
            pltpu.VMEM((2, YT, 8, BZ), F32),
            pltpu.VMEM((2, BY, BZ), F32),
            pltpu.VMEM((2, BX, 2 * NZT, 128), F32),
            pltpu.VMEM((2, BX, 2 * NZT, 128), F32),
            pltpu.VMEM((2, BX // 2, 2 * NZT, 128), F32),
            pltpu.VMEM((2, BX // 2, 2 * NZT, 128), F32),
            pltpu.VMEM((2, 16, 8, 128), F32),
            pltpu.SMEM((1, LISTED), jnp.int32),
            pltpu.VMEM((8, 6), jnp.int32),
            pltpu.SemaphoreType.DMA((CHUNKS + 1, 2 * NZT)),
            pltpu.SemaphoreType.DMA((60,)),
            pltpu.SemaphoreType.DMA((60,)),
        ],
        compiler_params=pltpu.CompilerParams(collective_id=0, has_side_effects=True, vmem_limit_bytes=38 * 2**20),
        cost_estimate=pl.CostEstimate(flops=80 * BX * BY * BZ, bytes_accessed=20 * 2**20, transcendentals=0),
        name="heat_steps",
    )(enthalpy.reshape(BX, YT, 8, BZ), conduct, tile_count, tile_list, neighbours)


def local(enthalpy, conduct, tile_count, tile_list, neighbours):
    h_new, shrink, old_l, new_l, table = heat_call(enthalpy, conduct, tile_count, tile_list, neighbours)
    return solve_call(h_new.reshape(BX, BY, BZ), shrink.reshape(BX, BY, BZ), old_l, new_l, table, tile_list)


def solution(mesh):
    placed = (
        P("grp", "dev", None),
        P("grp", "dev", None),
        P(("grp", "dev")),
        P(("grp", "dev"), None),
        P(("grp", "dev"), None),
    )
    return jax.shard_map(
        local,
        mesh=mesh,
        in_specs=placed,
        out_specs=(P("grp", "dev", None), P("grp", "dev", None), P("grp", "dev", None)),
        check_vma=False,
    )
```
